32 devices in a mesh: shard: 4 (over x, core), rep: 8 (over z, y).
Axes of the slice: x: 2, y: 2, z: 4, core: 2. Of those that a mesh axis runs over, the one named last changes fastest.
Arguments:
- tokens: bfloat16 [4096, 1024], P(('shard', 'rep')), may hold values from -6 to 6
- cotangent: bfloat16 [4096, 1024], P(('shard', 'rep')), may hold values from -6 to 6
- first_gain: bfloat16 [1024], P('shard'), may hold values from 0.099609375 to 1.8984375
- mixer_gate: bfloat16 [1024, 1536], P('shard'), may hold values from -0.1875 to 0.1875
- mixer_input: bfloat16 [1024, 1792], P('shard'), may hold values from -0.1875 to 0.1875
- step_weight: bfloat16 [1024, 24], P('shard'), may hold values from -0.1875 to 0.1875
- conv_weight: bfloat16 [4, 1792], P(None, 'shard'), may hold values from -3 to 3
- conv_bias: bfloat16 [1792], P('shard'), may hold values from -3 to 3
- step_bias: bfloat16 [24], P('shard'), may hold values from -6 to -2
- decay_log: bfloat16 [24], P('shard'), may hold values from 0 to 2.6875
- skip_weight: bfloat16 [24], P('shard'), may hold values from 0.5 to 2
- mixer_gain: bfloat16 [1536], P('shard'), may hold values from 0.099609375 to 1.8984375
- mixer_output: bfloat16 [1536, 1024], P('shard'), may hold values from -0.15625 to 0.15625
- query_matrix: bfloat16 [1024, 512], P('shard'), may hold values from -0.1875 to 0.1875
- key_matrix: bfloat16 [1024, 128], P('shard'), may hold values from -0.1875 to 0.1875
- value_matrix: bfloat16 [1024, 128], P('shard'), may hold values from -0.1875 to 0.1875
- attn_output: bfloat16 [512, 1024], P('shard'), may hold values from -1 to 1
- second_gain: bfloat16 [1024], P('shard'), may hold values from 0.099609375 to 1.8984375
- ffn_gate: bfloat16 [1024, 2048], P('shard'), may hold values from -0.1875 to 0.1875
- ffn_up: bfloat16 [1024, 2048], P('shard'), may hold values from -0.1875 to 0.1875
- ffn_down: bfloat16 [2048, 1024], P('shard'), may hold values from -0.125 to 0.125
Outputs:
- block_output: bfloat16 [4096, 1024], P(('shard', 'rep'))
- tokens_grad: bfloat16 [4096, 1024], P(('shard', 'rep'))
- grad_first_gain: float32 [1024], P(('shard', 'rep'))
- grad_mixer_gate: float32 [1024, 1536], P(('shard', 'rep'))
- grad_mixer_input: float32 [1024, 1792], P(('shard', 'rep'))
- grad_step_weight: float32 [1024, 24], P(('shard', 'rep'))
- grad_conv_weight: float32 [4, 1792], P(None, ('shard', 'rep'))
- grad_conv_bias: float32 [1792], P(('shard', 'rep'))
- grad_step_bias: float32 [24], P('shard')
- grad_decay_log: float32 [24], P('shard')
- grad_skip_weight: float32 [24], P('shard')
- grad_mixer_gain: float32 [1536], P(('shard', 'rep'))
- grad_mixer_output: float32 [1536, 1024], P(('shard', 'rep'))
- grad_query_weight: float32 [1024, 512], P(('shard', 'rep'))
- grad_key_weight: float32 [1024, 128], P(('shard', 'rep'))
- grad_value_weight: float32 [1024, 128], P(('shard', 'rep'))
- grad_attn_output: float32 [512, 1024], P(('shard', 'rep'))
- grad_second_gain: float32 [1024], P(('shard', 'rep'))
- grad_ffn_gate: float32 [1024, 2048], P(('shard', 'rep'))
- grad_ffn_up: float32 [1024, 2048], P(('shard', 'rep'))
- grad_ffn_down: float32 [2048, 1024], P(('shard', 'rep'))
The draws below stay inside these ranges and needn't reach their ends.
All inputs are finite; a program needn't handle non-finite values.
Results may differ from the reference program's by a relative error of at most 0.017.
Values may be sent and summed in bfloat16 or wider, within the bound.
No kernel may reach another device: no remote copies, remote signals or barrier semaphores. Data moves between devices by JAX's collectives and lax.ppermute only.
A program may use at most 192 MiB of HBM per device.

```python
import math
import jax
import jax.numpy as jnp
from jax import lax

MODEL_WIDTH = 1024
QUERY_HEADS = 8
KEY_VALUE_HEADS = 2
HEAD_WIDTH = 64
HM = 24
P_SIZE = 64
N = 128
KC = 4
FF = 2048
SEQUENCE_LENGTH = 128
DS = 1536
XBC = 1792
TOKENS = 4096


def shard_levels(stream_key, extent, cuts, smallest, top_value):
    def one(position, blocks):
        draws = jax.random.uniform(jax.random.fold_in(jax.random.fold_in(stream_key, 6), position), (blocks,), jnp.float32, smallest / len(cuts), top_value / len(cuts))
        return jnp.repeat(jnp.exp(draws), extent[position] // blocks).reshape((-1,) + (1,) * (len(extent) - position - 1))

    level = one(*cuts[0])
    for cut in cuts[1:]:
        level = level * one(*cut)
    return level


def normal_values(key, extent, deviation, reach, split=(), held_as=jnp.bfloat16):
    level = shard_levels(key, extent, split, -0.22, 0.18) if split else 1.0
    entries = jax.random.normal(key, extent, jnp.float32) * deviation * level
    return jnp.minimum(jnp.maximum(entries, -reach), reach).astype(held_as)


def setup_inputs(seed: int = 0) -> dict:
    streams_of = jax.random.split(jax.random.key(seed), 22)
    tokens = normal_values(streams_of[0], (TOKENS, MODEL_WIDTH), 1.0, 6.0, ((0, 32),))
    cotangent = normal_values(streams_of[1], (TOKENS, MODEL_WIDTH), 1.0, 6.0, ((0, 32),))
    first_gain = jnp.clip(1.0 + 0.18 * jax.random.normal(streams_of[2], (MODEL_WIDTH,), jnp.float32), 0.099609375, 1.8984375).astype(jnp.bfloat16)
    mixer_gate = normal_values(streams_of[3], (MODEL_WIDTH, DS), MODEL_WIDTH ** -0.5, 0.1875, ((0, 4),))
    mixer_input = normal_values(streams_of[4], (MODEL_WIDTH, XBC), MODEL_WIDTH ** -0.5, 0.1875, ((0, 4),))
    step_weight = normal_values(streams_of[5], (MODEL_WIDTH, HM), MODEL_WIDTH ** -0.5, 0.1875, ((0, 4),))
    conv_weight = normal_values(streams_of[6], (KC, XBC), 0.5, 3.0, ((1, 4),))
    conv_bias = normal_values(streams_of[7], (XBC,), 0.5, 3.0, ((0, 4),))
    step_bias = jnp.clip(-6.0 + 4.0 * jax.random.uniform(streams_of[8], (HM,), jnp.float32) ** shard_levels(streams_of[8], (HM,), ((0, 4),), -0.2, 0.2), -6.0, -2.0).astype(jnp.bfloat16)
    decay_log = jnp.clip(2.6875 * jax.random.uniform(streams_of[9], (HM,), jnp.float32) ** shard_levels(streams_of[9], (HM,), ((0, 4),), -0.2, 0.2), 0.0, 2.6875).astype(jnp.bfloat16)
    skip_weight = jnp.clip(0.5 + 1.5 * jax.random.uniform(streams_of[10], (HM,), jnp.float32) ** shard_levels(streams_of[10], (HM,), ((0, 4),), -0.2, 0.2), 0.5, 2.0).astype(jnp.bfloat16)
    mixer_gain = jnp.clip(1.0 + 0.18 * jax.random.normal(streams_of[11], (DS,), jnp.float32), 0.099609375, 1.8984375).astype(jnp.bfloat16)
    mixer_output = normal_values(streams_of[12], (DS, MODEL_WIDTH), DS ** -0.5, 0.15625, ((0, 4),))
    query_matrix = normal_values(streams_of[13], (MODEL_WIDTH, QUERY_HEADS * HEAD_WIDTH), MODEL_WIDTH ** -0.5, 0.1875, ((0, 4),))
    key_matrix = normal_values(streams_of[14], (MODEL_WIDTH, KEY_VALUE_HEADS * HEAD_WIDTH), MODEL_WIDTH ** -0.5, 0.1875, ((0, 4),))
    value_matrix = normal_values(streams_of[15], (MODEL_WIDTH, KEY_VALUE_HEADS * HEAD_WIDTH), MODEL_WIDTH ** -0.5, 0.1875, ((0, 4),))
    attn_output = normal_values(streams_of[16], (QUERY_HEADS * HEAD_WIDTH, MODEL_WIDTH), (QUERY_HEADS * HEAD_WIDTH // 16) ** -0.5, 1.0, ((0, 4),))
    second_gain = jnp.clip(1.0 + 0.18 * jax.random.normal(streams_of[17], (MODEL_WIDTH,), jnp.float32), 0.099609375, 1.8984375).astype(jnp.bfloat16)
    ffn_gate = normal_values(streams_of[18], (MODEL_WIDTH, FF), MODEL_WIDTH ** -0.5, 0.1875, ((0, 4),))
    ffn_up = normal_values(streams_of[19], (MODEL_WIDTH, FF), MODEL_WIDTH ** -0.5, 0.1875, ((0, 4),))
    ffn_down = normal_values(streams_of[20], (FF, MODEL_WIDTH), FF ** -0.5, 0.125, ((0, 4),))
    return {"tokens": tokens, "cotangent": cotangent, "first_gain": first_gain, "mixer_gate": mixer_gate, "mixer_input": mixer_input, "step_weight": step_weight, "conv_weight": conv_weight, "conv_bias": conv_bias, "step_bias": step_bias, "decay_log": decay_log, "skip_weight": skip_weight, "mixer_gain": mixer_gain, "mixer_output": mixer_output, "query_matrix": query_matrix, "key_matrix": key_matrix, "value_matrix": value_matrix, "attn_output": attn_output, "second_gain": second_gain, "ffn_gate": ffn_gate, "ffn_up": ffn_up, "ffn_down": ffn_down}


EPS = 1e-05
HIGH = lax.Precision.HIGHEST

@jax.custom_vjp
def low(v):
    return lax.optimization_barrier(v.astype(jnp.bfloat16)).astype(jnp.float32)

@jax.custom_vjp
def low_back(v):
    return v

def low_keep(v):
    return (low(v), None)

def low_pass(kept, grad):
    return (grad,)

def back_keep(v):
    return (v, None)

def back_low(kept, grad):
    return (low(grad),)
low.defvjp(low_keep, low_pass)
low_back.defvjp(back_keep, back_low)

def rounded_pair(value):
    return low(low_back(value))

def rms_scale(values, gain):
    return values * lax.rsqrt(lax.optimization_barrier(jnp.mean(values * values, axis=-1, keepdims=True)) + EPS) * gain

def apply_projection(inputs, weight):
    return jnp.einsum('bld,de->ble', inputs, weight, precision=HIGH)

def mixer_core(gate_in, mixed_in, step_in, kernel_taps, kernel_offset, step_offset, decay_rates, skip_scale, norm_gain):
    batch_count, token_length = (mixed_in.shape[0], mixed_in.shape[1])
    padded = jnp.pad(mixed_in, ((0, 0), (KC - 1, 0), (0, 0)))
    convolved = kernel_offset + padded[:, 0:token_length] * kernel_taps[0]
    for offset in range(1, KC):
        convolved = convolved + padded[:, offset:offset + token_length] * kernel_taps[offset]
    active = jax.nn.silu(convolved)
    inner_values = active[:, :, :DS].reshape(batch_count, token_length, HM, P_SIZE)
    in_state = active[:, :, DS:DS + N]
    out_state = active[:, :, DS + N:]
    step_size = jax.nn.softplus(step_in + step_offset)
    log_decay = -step_size * jnp.exp(decay_rates)
    running = jnp.cumsum(log_decay, axis=1)
    positions = jnp.arange(token_length)
    causal = (positions[:, None] >= positions[None, :])[None, :, :, None]
    spread = running[:, :, None, :] - running[:, None, :, :]
    decay_factor = jnp.where(causal, jnp.exp(jnp.where(causal, spread, 0.0)), 0.0)
    coupling = jnp.einsum('btn,bsn->bts', out_state, in_state, precision=HIGH)
    mixing = coupling[:, :, :, None] * decay_factor * step_size[:, None, :, :]
    result = jnp.einsum('btsh,bshp->bthp', mixing, inner_values, precision=HIGH) + skip_scale[:, None] * inner_values
    gated_values = result.reshape(batch_count, token_length, DS) * jax.nn.silu(gate_in)
    return rms_scale(gated_values, norm_gain)

def attention(query_head_rows, key_head_rows, value_head_rows):
    token_length = query_head_rows.shape[1]
    positions = jnp.arange(token_length)
    causal = positions[:, None] >= positions[None, :]
    raw = low_back(jnp.einsum('bqkjd,bskd->bkjqs', query_head_rows, key_head_rows, precision=HIGH))
    scores = jnp.where(causal, raw * HEAD_WIDTH ** (-0.5), -1e+30)
    shares = jax.nn.softmax(scores, axis=-1)
    return jnp.einsum('bkjqs,bskd->bqkjd', low(shares), value_head_rows, precision=HIGH)

def layer(weights, inputs):
    first_gain, mixer_gate, mixer_input, step_weight, conv_weight, conv_bias, step_bias, decay_log, skip_weight, mixer_gain, mixer_output, query_matrix, key_matrix, value_matrix, attn_output, second_gain, ffn_gate, ffn_up, ffn_down = weights
    batch_count, token_length = (inputs.shape[0], inputs.shape[1])
    normalized_input = low(rms_scale(inputs, first_gain))
    gate_in = low_back(apply_projection(normalized_input, mixer_gate))
    mixed_in = low_back(apply_projection(normalized_input, mixer_input))
    step_in = low_back(apply_projection(normalized_input, step_weight))
    mixer_norm = low(mixer_core(gate_in, mixed_in, step_in, conv_weight, conv_bias, step_bias, decay_log, skip_weight, mixer_gain))
    mixer_term = low_back(apply_projection(mixer_norm, mixer_output))
    query_head_rows = rounded_pair(apply_projection(normalized_input, query_matrix)).reshape(batch_count, token_length, KEY_VALUE_HEADS, QUERY_HEADS // KEY_VALUE_HEADS, HEAD_WIDTH)
    key_head_rows = rounded_pair(apply_projection(normalized_input, key_matrix)).reshape(batch_count, token_length, KEY_VALUE_HEADS, HEAD_WIDTH)
    value_head_rows = rounded_pair(apply_projection(normalized_input, value_matrix)).reshape(batch_count, token_length, KEY_VALUE_HEADS, HEAD_WIDTH)
    context = rounded_pair(attention(query_head_rows, key_head_rows, value_head_rows)).reshape(batch_count, token_length, QUERY_HEADS * HEAD_WIDTH)
    attn_term = low_back(apply_projection(context, attn_output))
    middle = inputs + mixer_term + attn_term
    normed_two = low(rms_scale(middle, second_gain))
    gate_value = low_back(apply_projection(normed_two, ffn_gate))
    up_value = low_back(apply_projection(normed_two, ffn_up))
    activated = low(jax.nn.silu(gate_value) * up_value)
    return middle + low_back(apply_projection(activated, ffn_down))

def reference(tokens, cotangent, first_gain, mixer_gate, mixer_input, step_weight, conv_weight, conv_bias, step_bias, decay_log, skip_weight, mixer_gain, mixer_output, query_matrix, key_matrix, value_matrix, attn_output, second_gain, ffn_gate, ffn_up, ffn_down):
    weights = tuple((weight.astype(jnp.float32) for weight in (first_gain, mixer_gate, mixer_input, step_weight, conv_weight, conv_bias, step_bias, decay_log, skip_weight, mixer_gain, mixer_output, query_matrix, key_matrix, value_matrix, attn_output, second_gain, ffn_gate, ffn_up, ffn_down)))
    sequences = tokens.shape[0] // SEQUENCE_LENGTH
    group_size = math.gcd(sequences, max(1, 4096 // SEQUENCE_LENGTH))
    rounds = sequences // group_size
    inputs = tokens.astype(jnp.float32).reshape(rounds, group_size, SEQUENCE_LENGTH, MODEL_WIDTH)
    cotangents = cotangent.astype(jnp.float32).reshape(rounds, group_size, SEQUENCE_LENGTH, MODEL_WIDTH)

    def advance(totals, pair):
        inputs_now, cotangent_now = pair
        outputs, pullback = jax.vjp(layer, weights, inputs_now)
        weight_grads, input_gradient = pullback(cotangent_now)
        totals = tuple((total + grad for total, grad in zip(totals, weight_grads)))
        return (totals, (outputs.astype(jnp.bfloat16), input_gradient.astype(jnp.bfloat16)))
    zeros = tuple((jnp.zeros_like(weight) for weight in weights))
    totals, (outputs, input_grads) = lax.scan(advance, zeros, (inputs, cotangents))
    return (outputs.reshape(tokens.shape), input_grads.reshape(tokens.shape), totals[0], totals[1], totals[2], totals[3], totals[4], totals[5], totals[6], totals[7], totals[8], totals[9], totals[10], totals[11], totals[12], totals[13], totals[14], totals[15], totals[16], totals[17], totals[18])
```

```python
import jax
import jax.numpy as jnp
from jax import lax
from jax.experimental import pallas as pl
from jax.experimental.pallas import tpu as pltpu
from jax.sharding import PartitionSpec as P

QUERY_HEADS = 8
KEY_VALUE_HEADS = 2
HEAD_WIDTH = 64
HM = 24
P_SIZE = 64
N = 128
KC = 4
SEQUENCE_LENGTH = 128
DS = 1536
XBC = 1792
WIDTH = 1024
QW = QUERY_HEADS * HEAD_WIDTH
KW = KEY_VALUE_HEADS * HEAD_WIDTH
GATE_AT, MIXED_AT = 0, DS
Q_AT = MIXED_AT + XBC
K_AT = Q_AT + QW
V_AT = K_AT + KW
STEP_AT = V_AT + KW
IN_COLS = STEP_AT + 128


EPS = 1e-05
HIGH = lax.Precision.HIGHEST
BF = jnp.bfloat16
F32 = jnp.float32


def rms_scale(values, gain):
    return values * lax.rsqrt(jnp.mean(values * values, axis=-1, keepdims=True) + EPS) * gain


def swiglu(gate_value, up_value):
    return jax.nn.silu(gate_value) * up_value


def mixer_core(
    gate_in,
    mixed_in,
    step_in,
    kernel_taps,
    kernel_offset,
    step_offset,
    decay_rates,
    skip_scale,
    norm_gain,
):
    batch_count, token_length = (mixed_in.shape[0], mixed_in.shape[1])
    padded = jnp.pad(mixed_in, ((0, 0), (KC - 1, 0), (0, 0)))
    convolved = kernel_offset + padded[:, 0:token_length] * kernel_taps[0]
    for offset in range(1, KC):
        convolved = convolved + padded[:, offset : offset + token_length] * kernel_taps[offset]
    active = jax.nn.silu(convolved)
    inner_values = active[:, :, :DS].reshape(batch_count, token_length, HM, P_SIZE)
    in_state = active[:, :, DS : DS + N]
    out_state = active[:, :, DS + N :]
    step_size = jax.nn.softplus(step_in + step_offset)
    log_decay = -step_size * jnp.exp(decay_rates)
    running = jnp.cumsum(log_decay, axis=1)
    positions = jnp.arange(token_length)
    causal = (positions[:, None] >= positions[None, :])[None, :, :, None]
    spread = running[:, :, None, :] - running[:, None, :, :]
    decay_factor = jnp.where(causal, jnp.exp(jnp.where(causal, spread, 0.0)), 0.0)
    coupling = jnp.einsum("btn,bsn->bts", out_state, in_state, precision=HIGH)
    mixing = coupling[:, :, :, None] * decay_factor * step_size[:, None, :, :]
    result = (
        jnp.einsum("btsh,bshp->bthp", mixing, inner_values, precision=HIGH)
        + skip_scale[:, None] * inner_values
    )
    gated_values = result.reshape(batch_count, token_length, DS) * jax.nn.silu(gate_in)
    return rms_scale(gated_values, norm_gain)


def matmul(left, right):
    return jnp.dot(left, right, preferred_element_type=F32)


def weight_grad(left, grad):
    return lax.dot_general(left, grad, (((0,), (0,)), ((), ())), preferred_element_type=F32)


def input_gradient(grad, weight):
    return lax.dot_general(grad, weight, (((1,), (1,)), ((), ())), preferred_element_type=F32)


def attention_scores(query_head_rows, key_head_rows, token_length):
    positions = jnp.arange(token_length)
    causal = positions[:, None] >= positions[None, :]
    raw = jnp.einsum(
        "bqkjd,bskd->bkjqs", query_head_rows, key_head_rows, preferred_element_type=F32
    )
    return jnp.where(causal, raw * HEAD_WIDTH ** (-0.5), -1e30)


def swap(value, axis, bit):
    size = lax.axis_size(axis)
    return lax.ppermute(value, axis, [(i, i ^ bit) for i in range(size)])


def core(value):
    return swap(value, "shard", 1)


def over_x(value):
    return swap(value, "shard", 2)


def over_y(value):
    return swap(value, "rep", 1)


def over_z(value):
    return swap(value, "rep", 2)


def place_kernel(count, offsets, *refs):
    pieces, out, sems = refs[:count], refs[count], refs[count + 1]
    copies = []
    for i, piece in enumerate(pieces):
        rows = piece.shape[0]
        start = pl.multiple_of(offsets[i], rows)
        copies.append(
            pltpu.make_async_copy(piece, out.at[pl.ds(start, rows)], sems.at[i])
        )
    for copy in copies:
        copy.start()
    for copy in copies:
        copy.wait()


def place(pieces, offsets, rows):
    count = len(pieces)
    columns = pieces[0].shape[1]

    def body(*refs):
        place_kernel(count, *refs)

    any_spec = pl.BlockSpec(memory_space=pl.ANY)
    return pl.pallas_call(
        body,
        out_shape=jax.ShapeDtypeStruct((rows, columns), pieces[0].dtype),
        in_specs=[pl.BlockSpec(memory_space=pltpu.SMEM)] + [any_spec] * count,
        out_specs=any_spec,
        scratch_shapes=[pltpu.SemaphoreType.DMA((count,))],
        name="place",
        cost_estimate=pl.CostEstimate(
            flops=0, bytes_accessed=4 * rows * columns, transcendentals=0
        ),
    )(jnp.stack([jnp.asarray(o, jnp.int32) for o in offsets]), *pieces)


def gather_weight(weight, shard, rep, quick):
    rows = weight.shape[0]
    part = rows // 4
    mine = rep & 3

    def quarter(j):
        return lax.dynamic_slice_in_dim(weight, j * part, part, 0)

    near = core(weight)
    far_x = over_x(quarter(mine))
    far_y = over_y(far_x)
    far_z = over_z(far_x)
    if quick:
        last = [(over_x(quarter(mine ^ 3)), 0)]
    else:
        half = part // 2
        last = [(over_y(far_z[:half]), 0), (over_z(far_y[half:]), half)]
    far = [(far_x, mine * part), (far_y, (mine ^ 1) * part), (far_z, (mine ^ 2) * part)]
    far += [(value, (mine ^ 3) * part + at) for value, at in last]
    pieces = [(weight, shard * rows), (near, (shard ^ 1) * rows)]
    pieces += [(value, (shard ^ 2) * rows + at) for value, at in far]
    pieces += [(core(value), (shard ^ 3) * rows + at) for value, at in far]
    return place([p for p, _ in pieces], [o for _, o in pieces], 4 * rows)


def group_rows(value):
    far = over_x(value)
    return jnp.concatenate([value, core(value), far, core(far)], axis=0)


def group_columns(value, shard):
    tokens = value.shape[0]
    split = value.reshape(tokens, 4, -1)

    def pick(j):
        return lax.dynamic_index_in_dim(split, j, 1, keepdims=False)

    far = over_x(pick(shard ^ 2))
    beyond = core(over_x(pick(shard ^ 3)))
    return jnp.concatenate([pick(shard), core(pick(shard ^ 1)), far, beyond], axis=0)


def bit_of(index, bit):
    return (index // bit) & 1


def reduce_rep(columns, grads, rep):
    reps = lax.axis_size("rep")
    tokens = columns.shape[0]
    mine = bit_of(rep, 1)
    split = columns.reshape(tokens, reps // 2, 2, -1)

    def pick(j):
        return lax.dynamic_index_in_dim(split, j, 2, keepdims=False).reshape(tokens, -1)

    arrived = over_y(weight_grad(pick(1 - mine), grads).astype(BF))
    total = weight_grad(pick(mine), grads) + arrived.astype(F32)
    bit, left = 2, reps // 2
    while left > 1:
        total = total.reshape(left // 2, 2, -1, total.shape[-1])
        mine = bit_of(rep, bit)
        sent = lax.dynamic_index_in_dim(total, 1 - mine, 1, keepdims=False)
        arrived = swap(sent.astype(BF), "rep", bit)
        total = lax.dynamic_index_in_dim(total, mine, 1, keepdims=False) + arrived.astype(F32)
        bit, left = bit * 2, left // 2
    return total.reshape(-1, total.shape[-1])


def reduce_small(blocks, shard, rep):
    total = blocks
    for axis, index, bit in (("shard", shard, 2), ("shard", shard, 1)):
        mine = bit_of(index, bit)
        total = total.reshape((2, -1) + blocks.shape[1:])
        arrived = swap(
            lax.dynamic_index_in_dim(total, 1 - mine, 0, keepdims=False), axis, bit
        )
        total = lax.dynamic_index_in_dim(total, mine, 0, keepdims=False) + arrived
    total = total.reshape(blocks.shape[1:])
    bit = lax.axis_size("rep") // 2
    while bit:
        mine = bit_of(rep, bit)
        total = total.reshape(2, -1, total.shape[-1])
        arrived = swap(
            lax.dynamic_index_in_dim(total, 1 - mine, 0, keepdims=False), "rep", bit
        )
        total = lax.dynamic_index_in_dim(total, mine, 0, keepdims=False) + arrived
        bit //= 2
    return total.reshape(-1)


def local(
    tokens,
    cotangent,
    first_gain,
    mixer_gate,
    mixer_input,
    step_weight,
    conv_weight,
    conv_bias,
    step_bias,
    decay_log,
    skip_weight,
    mixer_gain,
    mixer_output,
    query_matrix,
    key_matrix,
    value_matrix,
    attn_output,
    second_gain,
    ffn_gate,
    ffn_up,
    ffn_down,
):
    shard = lax.axis_index("shard")
    rep = lax.axis_index("rep")
    reps = lax.axis_size("rep")

    small_parts = (
        first_gain,
        conv_weight.reshape(-1),
        conv_bias,
        step_bias,
        decay_log,
        skip_weight,
        mixer_gain,
        second_gain,
    )
    small = jnp.concatenate(small_parts)
    small = jnp.pad(small, (0, -small.shape[0] % 128)).reshape(1, -1)
    far_small = over_x(small)
    smalls = jnp.concatenate([small, core(small), far_small, core(far_small)], axis=0)
    smalls = jnp.take(smalls, jnp.arange(4) ^ shard, axis=0).astype(F32)
    full, at = [], 0
    for part in small_parts:
        full.append(smalls[:, at : at + part.shape[0]])
        at += part.shape[0]
    taps = full[1].reshape(4, KC, -1).transpose(1, 0, 2).reshape(KC, XBC)
    gain_one, offset, step_offset, decay_rates, skip_scale, gain_mixer, gain_two = (
        full[i].reshape(-1) for i in (0, 2, 3, 4, 5, 6, 7)
    )

    step_padded = jnp.pad(step_weight, ((0, 0), (0, IN_COLS - STEP_AT - HM)))
    in_shard = jnp.concatenate(
        [mixer_gate, mixer_input, query_matrix, key_matrix, value_matrix, step_padded], axis=1
    )
    w_in = gather_weight(in_shard, shard, rep, True)
    w_out = gather_weight(jnp.concatenate([mixer_output, attn_output], axis=0), shard, rep, False)
    w_mid = gather_weight(jnp.concatenate([ffn_gate, ffn_up], axis=1), shard, rep, False)
    w_down = gather_weight(ffn_down, shard, rep, False)
    mixer_rows_of = DS // 4
    ff = w_mid.shape[1] // 2

    token_rows = tokens.shape[0]
    batch_count = token_rows // SEQUENCE_LENGTH
    shard_groups = QUERY_HEADS // KEY_VALUE_HEADS
    inputs = tokens.astype(F32)
    norm_one, norm_one_back = jax.vjp(rms_scale, inputs, gain_one)
    normalized_input = norm_one.astype(BF)
    projected = matmul(normalized_input, w_in)
    gate_in = projected[:, GATE_AT:MIXED_AT]
    mixed_in = projected[:, MIXED_AT:Q_AT]
    step_in = projected[:, STEP_AT : STEP_AT + HM]

    def mixer_rows(
        gate_part,
        mixed_part,
        step_part,
        kernel_taps,
        kernel_offset,
        step_offset,
        decay_rates,
        skip_scale,
        norm_gain,
    ):
        value = mixer_core(
            gate_part.reshape(batch_count, SEQUENCE_LENGTH, -1),
            mixed_part.reshape(batch_count, SEQUENCE_LENGTH, -1),
            step_part.reshape(batch_count, SEQUENCE_LENGTH, -1),
            kernel_taps,
            kernel_offset,
            step_offset,
            decay_rates,
            skip_scale,
            norm_gain,
        )
        return value.reshape(token_rows, -1)

    mixer_value, mixer_back = jax.vjp(
        mixer_rows,
        gate_in,
        mixed_in,
        step_in,
        taps,
        offset,
        step_offset,
        decay_rates,
        skip_scale,
        gain_mixer,
    )
    mixer_norm = mixer_value.astype(BF)
    query_reduced = projected[:, Q_AT:K_AT].astype(BF)
    key_reduced = projected[:, K_AT:V_AT].astype(BF)
    value_reduced = projected[:, V_AT:STEP_AT].astype(BF)
    query_head_rows = query_reduced.reshape(
        batch_count, SEQUENCE_LENGTH, KEY_VALUE_HEADS, shard_groups, HEAD_WIDTH
    )
    key_head_rows = key_reduced.reshape(batch_count, SEQUENCE_LENGTH, KEY_VALUE_HEADS, HEAD_WIDTH)
    value_head_rows = value_reduced.reshape(
        batch_count, SEQUENCE_LENGTH, KEY_VALUE_HEADS, HEAD_WIDTH
    )
    scores = attention_scores(query_head_rows, key_head_rows, SEQUENCE_LENGTH)
    row_top = jnp.max(scores, axis=-1, keepdims=True)
    unscaled = jnp.exp(scores - row_top)
    row_total = jnp.sum(unscaled, axis=-1, keepdims=True)
    shares = unscaled / row_total
    shares_low = shares.astype(BF)
    context = jnp.einsum(
        "bkjqs,bskd->bqkjd", shares_low, value_head_rows, preferred_element_type=F32
    )
    context_low = context.reshape(token_rows, QW).astype(BF)
    out_side = jnp.concatenate(
        [mixer_norm.reshape(token_rows, 4, -1), context_low.reshape(token_rows, 4, -1)], axis=2
    ).reshape(token_rows, -1)
    middle = inputs + matmul(out_side, w_out)
    norm_two, norm_two_back = jax.vjp(rms_scale, middle, gain_two)
    normed_two = norm_two.astype(BF)
    mid = matmul(normed_two, w_mid)
    activated, swiglu_back = jax.vjp(swiglu, mid[:, :ff], mid[:, ff:])
    activated_low = activated.astype(BF)
    output = (middle + matmul(activated_low, w_down)).astype(BF)

    grad_activated = input_gradient(cotangent, w_down)
    grad_gate_wide, grad_up_wide = swiglu_back(grad_activated)
    grad_mid = jnp.concatenate([grad_gate_wide, grad_up_wide], axis=1).astype(BF)
    grad_normed_two = input_gradient(grad_mid, w_mid)
    grad_middle_norm, grad_gain_two = norm_two_back(grad_normed_two)
    grad_middle = cotangent.astype(F32) + grad_middle_norm
    branch_gradient = grad_middle.astype(BF)
    grad_out_side = input_gradient(branch_gradient, w_out).reshape(token_rows, 4, -1)
    grad_mixer_norm = grad_out_side[:, :, :mixer_rows_of].reshape(token_rows, DS)
    grad_context = (
        grad_out_side[:, :, mixer_rows_of:]
        .astype(BF)
        .reshape(batch_count, SEQUENCE_LENGTH, KEY_VALUE_HEADS, shard_groups, HEAD_WIDTH)
    )
    grad_shares = jnp.einsum(
        "bqkjd,bskd->bkjqs", grad_context, value_head_rows, preferred_element_type=F32
    )
    value_gradient_full = jnp.einsum(
        "bkjqs,bqkjd->bskd", shares_low, grad_context, preferred_element_type=F32
    )
    grad_scores = shares * (grad_shares - jnp.sum(shares * grad_shares, axis=-1, keepdims=True))
    grad_raw = (grad_scores * HEAD_WIDTH ** (-0.5)).astype(BF)
    grad_query_wide = jnp.einsum(
        "bkjqs,bskd->bqkjd", grad_raw, key_head_rows, preferred_element_type=F32
    )
    key_gradient_full = jnp.einsum(
        "bkjqs,bqkjd->bskd", grad_raw, query_head_rows, preferred_element_type=F32
    )
    (
        grad_gate_in,
        grad_mixed_in,
        grad_step_in,
        grad_taps,
        grad_offset,
        grad_step_offset,
        grad_decay,
        grad_skip,
        grad_gain_mixer,
    ) = mixer_back(grad_mixer_norm)
    grad_projected = jnp.concatenate(
        [
            grad_gate_in.astype(BF),
            grad_mixed_in.astype(BF),
            grad_query_wide.reshape(token_rows, QW).astype(BF),
            key_gradient_full.reshape(token_rows, KW).astype(BF),
            value_gradient_full.reshape(token_rows, KW).astype(BF),
            jnp.pad(grad_step_in.astype(BF), ((0, 0), (0, IN_COLS - STEP_AT - HM))),
        ],
        axis=1,
    )
    grad_normed = input_gradient(grad_projected, w_in)
    grad_inputs_norm, grad_gain_one = norm_one_back(grad_normed)
    tokens_grad = (grad_middle + grad_inputs_norm).astype(BF)

    down = reduce_rep(group_columns(activated_low, shard), group_rows(cotangent), rep)
    mid_grad = reduce_rep(group_columns(normed_two, shard), group_rows(grad_mid), rep)
    out_columns = group_columns(out_side, shard)
    group_tokens = out_columns.shape[0]
    out_columns = jnp.concatenate(
        [
            out_columns[:, :mixer_rows_of].reshape(group_tokens, reps, -1),
            out_columns[:, mixer_rows_of:].reshape(group_tokens, reps, -1),
        ],
        axis=2,
    ).reshape(group_tokens, -1)
    out_grad = reduce_rep(out_columns, group_rows(branch_gradient), rep)
    in_grad = reduce_rep(group_columns(normalized_input, shard), group_rows(grad_projected), rep)

    def blocks(vector):
        return vector.reshape(4, reps, -1)

    heads = jnp.concatenate(
        [grad_step_offset.reshape(4, -1), grad_decay.reshape(4, -1), grad_skip.reshape(4, -1)],
        axis=1,
    )
    small_grads = (
        blocks(grad_gain_one),
        grad_taps.reshape(KC, 4, reps, -1).transpose(1, 2, 0, 3).reshape(4, reps, -1),
        blocks(grad_offset),
        blocks(grad_gain_mixer),
        blocks(grad_gain_two),
        jnp.broadcast_to(heads[:, None, :], (4, reps, heads.shape[1])),
    )
    small_total = reduce_small(jnp.concatenate(small_grads, axis=2), shard, rep)
    smalls_out, at = [], 0
    for part in small_grads:
        smalls_out.append(small_total[at : at + part.shape[2]])
        at += part.shape[2]
    gain_one_out, taps_out, offset_out, gain_mixer_out, gain_two_out, heads_out = smalls_out
    each = HM // 4
    mixer_m = mixer_rows_of // reps
    return (
        output,
        tokens_grad,
        gain_one_out,
        in_grad[:, GATE_AT:MIXED_AT],
        in_grad[:, MIXED_AT:Q_AT],
        in_grad[:, STEP_AT : STEP_AT + HM],
        taps_out.reshape(KC, -1),
        offset_out,
        heads_out[:each],
        heads_out[each : 2 * each],
        heads_out[2 * each :],
        gain_mixer_out,
        out_grad[:mixer_m],
        in_grad[:, Q_AT:K_AT],
        in_grad[:, K_AT:V_AT],
        in_grad[:, V_AT:STEP_AT],
        out_grad[mixer_m:],
        gain_two_out,
        mid_grad[:, :ff],
        mid_grad[:, ff:],
        down,
    )


def solution(mesh):
    both = P(("shard", "rep"), None)
    rows, vector = P("shard", None), P("shard")
    owned = P(("shard", "rep"))
    return jax.shard_map(
        local,
        mesh=mesh,
        in_specs=(
            both,
            both,
            vector,
            rows,
            rows,
            rows,
            P(None, "shard"),
            vector,
            vector,
            vector,
            vector,
            vector,
            rows,
            rows,
            rows,
            rows,
            rows,
            vector,
            rows,
            rows,
            rows,
        ),
        out_specs=(
            both,
            both,
            owned,
            both,
            both,
            both,
            P(None, ("shard", "rep")),
            owned,
            vector,
            vector,
            vector,
            owned,
            both,
            both,
            both,
            both,
            both,
            owned,
            both,
            both,
            both,
        ),
        check_vma=False,
    )
```

```python
import jax
import jax.numpy as jnp
from jax import lax
from jax.experimental import pallas as pl
from jax.experimental.pallas import tpu as pltpu
from jax.sharding import PartitionSpec as P

QUERY_HEADS = 8
KEY_VALUE_HEADS = 2
HEAD_WIDTH = 64
HM = 24
P_SIZE = 64
N = 128
KC = 4
SEQUENCE_LENGTH = 128
DS = 1536
XBC = 1792
WIDTH = 1024
QW = QUERY_HEADS * HEAD_WIDTH
KW = KEY_VALUE_HEADS * HEAD_WIDTH
GATE_AT, MIXED_AT = 0, DS
Q_AT = MIXED_AT + XBC
K_AT = Q_AT + QW
V_AT = K_AT + KW
STEP_AT = V_AT + KW
IN_COLS = STEP_AT + 128


EPS = 1e-05
HIGH = lax.Precision.HIGHEST
BF = jnp.bfloat16
F32 = jnp.float32


def swap(value, axis, bit):
    size = lax.axis_size(axis)
    return lax.ppermute(value, axis, [(i, i ^ bit) for i in range(size)])


def core(value):
    return swap(value, "shard", 1)


def over_x(value):
    return swap(value, "shard", 2)


def over_y(value):
    return swap(value, "rep", 1)


def over_z(value):
    return swap(value, "rep", 2)


def over_zz(value):
    return swap(value, "rep", 4)


ANY = pl.BlockSpec(memory_space=pltpu.HBM)
VMEM = pl.BlockSpec(memory_space=pltpu.VMEM)
SMEM = pl.BlockSpec(memory_space=pltpu.SMEM)
VMEM_LIMIT = 60 << 20


def call(body, outs, in_specs, scratch, name, flops=0, moved=0):
    return pl.pallas_call(
        body,
        out_shape=[jax.ShapeDtypeStruct(shape, dtype) for shape, dtype in outs],
        in_specs=in_specs,
        out_specs=[VMEM] * len(outs),
        scratch_shapes=scratch,
        compiler_params=pltpu.CompilerParams(vmem_limit_bytes=VMEM_LIMIT),
        name=name,
        cost_estimate=pl.CostEstimate(flops=0, bytes_accessed=0, transcendentals=0),
    )


def run_copies(pairs, sems):
    copies = [
        pltpu.make_async_copy(source, target, sems.at[i]) for i, (source, target) in enumerate(pairs)
    ]
    for copy in copies:
        copy.start()
    for copy in copies:
        copy.wait()


def after(value, *others):
    def body(*refs):
        del refs

    return pl.pallas_call(
        body,
        out_shape=jax.ShapeDtypeStruct(value.shape, value.dtype),
        in_specs=[ANY] * (1 + len(others)),
        out_specs=ANY,
        input_output_aliases={0: 0},
        name="after",
    )(value, *others)


def dot(left, right):
    return jnp.dot(left, right, preferred_element_type=F32)


def dot_rows(left, right):
    return lax.dot_general(left, right, (((1,), (1,)), ((), ())), preferred_element_type=F32)


def dot_tokens(left, right):
    return lax.dot_general(left, right, (((0,), (0,)), ((), ())), preferred_element_type=F32)


def quarter(meta, rows):
    part = rows // 4
    return part, pl.multiple_of((meta[1] & 3) * part, part)


IN_PARTS = (
    (GATE_AT, DS),
    (MIXED_AT, XBC),
    (Q_AT, QW),
    (K_AT, KW),
    (V_AT, KW),
)


def pack_in_quarter(meta, step, mixer_gate, mixer_input, query, key, value):
    rows = step.shape[0]

    def body(meta, step, *refs):
        weights, (target, sems) = refs[:5], refs[5:]
        part, start = quarter(meta, rows)
        target[:, STEP_AT:] = jnp.zeros((part, IN_COLS - STEP_AT), BF)
        target[:, STEP_AT : STEP_AT + HM] = step[pl.ds(start, part), :]
        run_copies(
            [
                (weight.at[pl.ds(start, part)], target.at[:, pl.ds(at, width)])
                for (at, width), weight in zip(IN_PARTS, weights)
            ],
            sems,
        )

    return call(
        body,
        [((rows // 4, IN_COLS), BF)],
        [SMEM, VMEM] + [ANY] * 5,
        [pltpu.SemaphoreType.DMA((5,))],
        "pack_in_quarter",
    )(meta, step, mixer_gate, mixer_input, query, key, value)[0]


def pack_in(step, mixer_gate, mixer_input, query, key, value):
    rows = step.shape[0]

    def body(step, *refs):
        weights, (target, sems) = refs[:5], refs[5:]
        target[:, STEP_AT:] = jnp.zeros((rows, IN_COLS - STEP_AT), BF)
        target[:, STEP_AT : STEP_AT + HM] = step[...]
        run_copies(
            [
                (weight, target.at[:, pl.ds(at, width)])
                for (at, width), weight in zip(IN_PARTS, weights)
            ],
            sems,
        )

    return call(
        body,
        [((rows, IN_COLS), BF)],
        [VMEM] + [ANY] * 5,
        [pltpu.SemaphoreType.DMA((5,))],
        "pack_in",
        moved=4 * rows * IN_COLS,
    )(step, mixer_gate, mixer_input, query, key, value)[0]


OUT_AT, FFN_GATE_AT, FFN_UP_AT, DOWN_AT = 0, 2048, 4096, 6144
REST_COLS = 8192


def pack_rest(meta, behind, mixer_output, attn_output, gate, up, down):
    rows = gate.shape[0]
    half = rows // 2

    def body(meta, behind, mixer_output, attn_output, gate, up, down, target, first, sems):
        def block(at, width=WIDTH):
            return target.at[:, pl.ds(at, width)]

        low = target.at[pl.ds(0, half), pl.ds(OUT_AT + WIDTH, WIDTH)]
        high = target.at[pl.ds(half, half), pl.ds(OUT_AT + WIDTH, WIDTH)]
        pairs = [
            (mixer_output.at[pl.ds(0, rows)], block(OUT_AT)),
            (gate, block(FFN_GATE_AT, 2048)),
            (up, block(FFN_UP_AT, 2048)),
            (down.at[pl.ds(0, rows)], block(DOWN_AT)),
            (down.at[pl.ds(rows, rows)], block(DOWN_AT + WIDTH)),
            (mixer_output.at[pl.ds(rows, half)], low),
            (attn_output, high),
        ]
        run_copies(pairs, sems)
        part, start = quarter(meta, rows)
        first[...] = target[pl.ds(start, part), :]

    return call(
        body,
        [((rows, REST_COLS), BF), ((rows // 4, REST_COLS), BF)],
        [SMEM] + [ANY] * 6,
        [pltpu.SemaphoreType.DMA((7,))],
        "pack_rest",
    )(meta, behind, mixer_output, attn_output, gate, up, down)


def spread(packed, near, first, last):
    half = first.shape[0] // 2
    from_y, from_z = over_y(first), over_z(first)
    low, high = over_y(from_z[:half]), over_z(from_y[half:])
    far = (first, from_y, from_z, after(low, last), after(high, last))
    return (packed, near) + far + tuple(core(piece) for piece in far)


def spread_first(first, *others):
    first = after(first, *others)
    return first, over_y(first), over_z(first)


def spread_last(packed, near, parts, middle, end):
    first, from_y, from_z = parts
    half = first.shape[0] // 2
    from_y, from_z = after(from_y, middle), after(from_z, middle)
    low, high = over_y(from_z[:half]), over_z(from_y[half:])
    far = (first, from_y, from_z, low, high)
    others = tuple(core(piece) for piece in far[:3])
    low, high = after(low, end), after(high, end)
    return (packed, near, first, from_y, from_z, low, high) + others + (core(low), core(high))


def fill(meta, pieces, target, sems):
    shard, mine = meta[0], meta[1] & 3
    rows = pieces[0].shape[0]
    part = rows // 4
    pairs = [
        (pieces[0], target.at[pl.ds(pl.multiple_of(shard * rows, rows), rows)]),
        (pieces[1], target.at[pl.ds(pl.multiple_of((shard ^ 1) * rows, rows), rows)]),
    ]
    for at, owner in ((2, shard ^ 2), (7, shard ^ 3)):
        for j, add in enumerate((0, 0, 0, 0, part // 2)):
            start = pl.multiple_of(owner * rows + (mine ^ min(j, 3)) * part + add, part // 2)
            size = part if j < 3 else part // 2
            pairs.append((pieces[at + j], target.at[pl.ds(start, size)]))
    run_copies(pairs, sems)


PIECES = 12
MIX_SHARD, ATT_SHARD, FF_SHARD, W_SHARD = DS // 4, QW // 4, 512, WIDTH // 4
OUT_SHARD = MIX_SHARD + ATT_SHARD


def columns_of(ref, shard, width):
    return ref[:, pl.ds(pl.multiple_of(shard * width, 128), width)]


def columns_for_others(shard, ref, width, to_x, to_core, at=0):
    to_x[:, at : at + width] = columns_of(ref, shard ^ 2, width)
    to_x[:, at + width : at + 2 * width] = columns_of(ref, shard ^ 3, width)
    to_core[:, at : at + width] = columns_of(ref, shard ^ 1, width)


def norm_rate(value):
    return lax.rsqrt(jnp.mean(value * value, axis=-1, keepdims=True) + EPS)


def norm_back(value, rate, gain, grad):
    scaled = gain * grad
    grad_value = rate * scaled - value * (rate * rate * rate) * jnp.mean(
        value * scaled, axis=-1, keepdims=True
    )
    return grad_value, jnp.sum(value * rate * grad, axis=0, keepdims=True)


def project_in(meta, tokens, gain, pieces):
    def body(meta, tokens, gain, *refs):
        pieces, (normed_ref, to_x, to_core, out, weight, sems) = refs[:PIECES], refs[PIECES:]
        fill(meta, pieces, weight, sems)
        value = tokens[...].astype(F32)
        normed = (value * norm_rate(value) * gain[...]).astype(BF)
        normed_ref[...] = normed
        columns_for_others(meta[0], normed_ref, W_SHARD, to_x, to_core)
        out[...] = dot(normed, weight[...])

    rows = tokens.shape[0]
    return call(
        body,
        [
            ((rows, WIDTH), BF),
            ((rows, 2 * W_SHARD), BF),
            ((rows, W_SHARD), BF),
            ((rows, IN_COLS), F32),
        ],
        [SMEM, VMEM, VMEM] + [ANY] * PIECES,
        [pltpu.VMEM((WIDTH, IN_COLS), BF), pltpu.SemaphoreType.DMA((PIECES,))],
        "project_in",
        flops=2 * rows * WIDTH * IN_COLS,
        moved=2 * WIDTH * IN_COLS,
    )(meta, tokens, gain, *pieces)


def project_in_back(meta, tokens, gain, grad_projected, grad_middle, pieces):
    def body(meta, tokens, gain, grad_projected, grad_middle, *refs):
        pieces, (out, grad_gain, weight, sems) = refs[:PIECES], refs[PIECES:]
        fill(meta, pieces, weight, sems)
        value = tokens[...].astype(F32)
        rate = norm_rate(value)
        grad = dot_rows(grad_projected[:, :IN_COLS], weight[...])
        grad_value, grad_gain[...] = norm_back(value, rate, gain[...], grad)
        out[...] = (grad_middle[...] + grad_value).astype(BF)

    rows = tokens.shape[0]
    return call(
        body,
        [((rows, WIDTH), BF), ((1, WIDTH), F32)],
        [SMEM] + [VMEM] * 4 + [ANY] * PIECES,
        [pltpu.VMEM((WIDTH, IN_COLS), BF), pltpu.SemaphoreType.DMA((PIECES,))],
        "project_in_back",
        flops=2 * rows * WIDTH * IN_COLS,
        moved=2 * WIDTH * IN_COLS,
    )(meta, tokens, gain, grad_projected, grad_middle, *pieces)


def silu_parts(value):
    share = 1.0 / (1.0 + jnp.exp(-value))
    return value * share, share


def silu_slope(value, share):
    return share * (1.0 + value * (1.0 - share))


def exact(left, right, axes=((1,), (0,))):
    return lax.dot_general(
        left, right, (axes, ((), ())), precision=HIGH, preferred_element_type=F32
    )


def causal_mask(rows):
    return lax.broadcasted_iota(jnp.int32, (rows, rows), 0) >= lax.broadcasted_iota(
        jnp.int32, (rows, rows), 1
    )


EDGE = 8


def mixer_state(projected, taps, offset, step_offset, decay, padded, causal):
    rows = projected.shape[0]
    padded[:EDGE] = jnp.zeros((EDGE, XBC), F32)
    padded[EDGE:] = projected[:, MIXED_AT:Q_AT]
    convolved = offset[...]
    for o in range(KC):
        start = EDGE - KC + 1 + o
        convolved = convolved + padded[start : start + rows] * taps[o : o + 1]
    active, share = silu_parts(convolved)
    raw = projected[:, STEP_AT:] + step_offset[...]
    step = jnp.maximum(raw, 0.0) + jnp.log1p(jnp.exp(-jnp.abs(raw)))
    rate = jnp.exp(decay[...])
    log_decay = -step * rate
    running = exact(causal.astype(F32), log_decay)
    return convolved, active, share, raw, step, rate, log_decay, running


def decay_of(running, running_t, causal, h):
    spread = running[:, h : h + 1] - running_t[h : h + 1]
    return jnp.where(causal, jnp.exp(jnp.where(causal, spread, 0.0)), 0.0)


def head(value, h):
    return value[:, h * HEAD_WIDTH : (h + 1) * HEAD_WIDTH]


def shares_of(query, key, causal):
    scores = jnp.where(causal, dot_rows(query, key) * HEAD_WIDTH ** (-0.5), -1e30)
    unscaled = jnp.exp(scores - jnp.max(scores, axis=-1, keepdims=True))
    return unscaled / jnp.sum(unscaled, axis=-1, keepdims=True)


def mix(meta, projected, taps, offset, step_offset, decay, skip, gain):
    rows = projected.shape[0]

    def body(meta, projected, taps, offset, step_offset, decay, skip, gain, *refs):
        side, to_x, to_core, result_ref, padded, active_ref = refs
        causal = causal_mask(rows)
        _, active, _, _, step, _, _, running = mixer_state(
            projected, taps, offset, step_offset, decay, padded, causal
        )
        active_ref[...] = active
        running_t, step_t = running.T, step.T
        coupling = exact(active[:, DS + N :], active[:, DS : DS + N], ((1,), (1,)))
        for h in range(HM):
            mixing = coupling * decay_of(running, running_t, causal, h) * step_t[h : h + 1]
            at = h * P_SIZE
            result_ref[:, at : at + P_SIZE] = exact(mixing, active_ref[:, at : at + P_SIZE])
        result = result_ref[...] + skip[...] * active_ref[:, :DS]
        gated = result * silu_parts(projected[:, GATE_AT:MIXED_AT])[0]
        mixed = (gated * norm_rate(gated) * gain[...]).astype(BF)
        for k in range(4):
            side[:, k * OUT_SHARD : k * OUT_SHARD + MIX_SHARD] = mixed[
                :, k * MIX_SHARD : (k + 1) * MIX_SHARD
            ]
        for h in range(QUERY_HEADS):
            query = projected[:, Q_AT + h * HEAD_WIDTH : Q_AT + (h + 1) * HEAD_WIDTH]
            at = (h // (QUERY_HEADS // KEY_VALUE_HEADS)) * HEAD_WIDTH
            key = projected[:, K_AT + at : K_AT + at + HEAD_WIDTH]
            value = projected[:, V_AT + at : V_AT + at + HEAD_WIDTH]
            shares = shares_of(query.astype(BF), key.astype(BF), causal)
            at = (h // 2) * OUT_SHARD + MIX_SHARD + (h % 2) * HEAD_WIDTH
            side[:, at : at + HEAD_WIDTH] = dot(shares.astype(BF), value.astype(BF)).astype(BF)
        columns_for_others(meta[0], side, OUT_SHARD, to_x, to_core)

    return call(
        body,
        [((rows, 4 * OUT_SHARD), BF), ((rows, 2 * OUT_SHARD), BF), ((rows, OUT_SHARD), BF)],
        [SMEM] + [VMEM] * 7,
        [
            pltpu.VMEM((rows, DS), F32),
            pltpu.VMEM((EDGE + rows, XBC), F32),
            pltpu.VMEM((rows, XBC), F32),
        ],
        "mix",
    )(meta, projected, taps, offset, step_offset, decay, skip, gain)


def mix_back(projected, taps, offset, step_offset, decay, skip, gain, grad_norm, grad_ctx):
    rows = projected.shape[0]

    def body(projected, taps, offset, step_offset, decay, skip, gain, grad_norm, grad_ctx, *refs):
        (
            to_core,
            grad_gain,
            grad_taps,
            grad_offset,
            grad_step_offset,
            grad_decay,
            grad_skip,
            result_ref,
            padded,
            active_ref,
            grad_active,
            column_ref,
            row_ref,
        ) = refs
        causal = causal_mask(rows)
        convolved, active, share, raw, step, rate, log_decay, running = mixer_state(
            projected, taps, offset, step_offset, decay, padded, causal
        )
        active_ref[...] = active
        running_t, step_t = running.T, step.T
        in_state, out_state = active[:, DS : DS + N], active[:, DS + N :]
        coupling = exact(out_state, in_state, ((1,), (1,)))
        for h in range(HM):
            mixing = coupling * decay_of(running, running_t, causal, h) * step_t[h : h + 1]
            at = h * P_SIZE
            result_ref[:, at : at + P_SIZE] = exact(mixing, active_ref[:, at : at + P_SIZE])
        inner = active_ref[:, :DS]
        result = result_ref[...] + skip[...] * inner
        gate = projected[:, GATE_AT:MIXED_AT]
        silu, gate_share = silu_parts(gate)
        gated = result * silu
        grad_gated, grad_gain[...] = norm_back(gated, norm_rate(gated), gain[...], grad_norm[...])
        to_core[:, GATE_AT:MIXED_AT] = (
            grad_gated * result * silu_slope(gate, gate_share)
        ).astype(BF)
        grad_result = grad_gated * silu
        result_ref[...] = grad_result
        grad_skip[...] = jnp.sum(grad_result * inner, axis=0, keepdims=True)
        grad_coupling = jnp.zeros((rows, rows), F32)
        column_ref[...] = jnp.zeros_like(column_ref)
        row_ref[...] = jnp.zeros_like(row_ref)
        for h in range(HM):
            at = h * P_SIZE
            decays = decay_of(running, running_t, causal, h)
            step_row = step_t[h : h + 1]
            scaled = decays * step_row
            grad_out = result_ref[:, at : at + P_SIZE]
            grad_active[:, at : at + P_SIZE] = exact(coupling * scaled, grad_out, ((0,), (0,)))
            grad_mixing = exact(grad_out, active_ref[:, at : at + P_SIZE], ((1,), (1,)))
            grad_coupling = grad_coupling + grad_mixing * scaled
            weighed = grad_mixing * decays * coupling
            row_ref[h : h + 1] = jnp.sum(weighed, axis=0, keepdims=True)
            column_ref[:, h : h + 1] = jnp.sum(weighed * step_row, axis=1, keepdims=True)
        grad_active[:, :DS] = grad_active[:, :DS] + skip[...] * result_ref[...]
        grad_active[:, DS : DS + N] = exact(grad_coupling, out_state, ((0,), (0,)))
        grad_active[:, DS + N :] = exact(grad_coupling, in_state)
        grad_step = row_ref[...].T
        grad_running = column_ref[...] - grad_step * step
        grad_log = exact(causal.astype(F32), grad_running, ((0,), (0,)))
        grad_decay[...] = jnp.sum(grad_log * log_decay, axis=0, keepdims=True)
        grad_raw = (grad_step - grad_log * rate) / (1.0 + jnp.exp(-raw))
        grad_step_offset[...] = jnp.sum(grad_raw, axis=0, keepdims=True)
        lanes = lax.broadcasted_iota(jnp.int32, (rows, 128), 1)
        to_core[:, STEP_AT:IN_COLS] = jnp.where(lanes < HM, grad_raw, 0.0).astype(BF)
        grad_conv = grad_active[...] * silu_slope(convolved, share)
        grad_offset[...] = jnp.sum(grad_conv, axis=0, keepdims=True)
        for o in range(KC):
            start = EDGE - KC + 1 + o
            grad_taps[o : o + 1] = jnp.sum(
                grad_conv * padded[start : start + rows], axis=0, keepdims=True
            )
        padded[:rows] = grad_conv
        padded[rows:] = jnp.zeros((EDGE, XBC), F32)
        grad_mixed = grad_conv * taps[KC - 1 : KC]
        for o in range(KC - 1):
            start = KC - 1 - o
            grad_mixed = grad_mixed + padded[start : start + rows] * taps[o : o + 1]
        to_core[:, MIXED_AT:Q_AT] = grad_mixed.astype(BF)

        group = QUERY_HEADS // KEY_VALUE_HEADS
        for kv in range(KEY_VALUE_HEADS):
            at = kv * HEAD_WIDTH
            key = projected[:, K_AT + at : K_AT + at + HEAD_WIDTH].astype(BF)
            value = projected[:, V_AT + at : V_AT + at + HEAD_WIDTH].astype(BF)
            grad_key = jnp.zeros((rows, HEAD_WIDTH), F32)
            grad_value = jnp.zeros((rows, HEAD_WIDTH), F32)
            for h in range(kv * group, (kv + 1) * group):
                query = projected[:, Q_AT + h * HEAD_WIDTH : Q_AT + (h + 1) * HEAD_WIDTH]
                query = query.astype(BF)
                shares = shares_of(query, key, causal)
                given = grad_ctx[:, h * HEAD_WIDTH : (h + 1) * HEAD_WIDTH]
                grad_shares = dot_rows(given, value)
                grad_value = grad_value + dot_tokens(shares.astype(BF), given)
                weighed = shares * grad_shares
                grad_scores = weighed - shares * jnp.sum(weighed, axis=-1, keepdims=True)
                grad_scores = (grad_scores * HEAD_WIDTH ** (-0.5)).astype(BF)
                to_core[:, Q_AT + h * HEAD_WIDTH : Q_AT + (h + 1) * HEAD_WIDTH] = dot(
                    grad_scores, key
                ).astype(BF)
                grad_key = grad_key + dot_tokens(grad_scores, query)
            to_core[:, K_AT + at : K_AT + at + HEAD_WIDTH] = grad_key.astype(BF)
            to_core[:, V_AT + at : V_AT + at + HEAD_WIDTH] = grad_value.astype(BF)
    return call(
        body,
        [
            ((rows, IN_COLS), BF),
            ((1, DS), F32),
            ((KC, XBC), F32),
            ((1, XBC), F32),
            ((1, 128), F32),
            ((1, 128), F32),
            ((1, DS), F32),
        ],
        [VMEM] * 9,
        [
            pltpu.VMEM((rows, DS), F32),
            pltpu.VMEM((EDGE + rows, XBC), F32),
            pltpu.VMEM((rows, XBC), F32),
            pltpu.VMEM((rows, XBC), F32),
            pltpu.VMEM((rows, 128), F32),
            pltpu.VMEM((128, rows), F32),
        ],
        "mix_back",
    )(projected, taps, offset, step_offset, decay, skip, gain, grad_norm, grad_ctx)


def feed_forward(meta, tokens, cotangent, side, gain, pieces):
    def body(meta, tokens, cotangent, side, gain, *refs):
        pieces, refs = refs[:PIECES], refs[PIECES:]
        (
            output,
            normed_ref,
            act_ref,
            grad_middle_ref,
            grad_norm_ref,
            grad_context_ref,
            grad_gain,
            mid_x,
            mid_core,
            rest_x,
            rest_core,
            weight,
            sems,
        ) = refs
        fill(meta, pieces, weight, sems)
        shard = meta[0]

        def block(at):
            return weight[:, at : at + WIDTH]

        def half_of(ref, h):
            return jnp.concatenate(
                [ref[:, k * 512 + h * 256 : k * 512 + h * 256 + 256] for k in range(4)], axis=1
            )

        middle = tokens[...].astype(F32)
        for h in range(2):
            middle = middle + dot(half_of(side, h), block(OUT_AT + h * WIDTH))
        rate = norm_rate(middle)
        normed = (middle * rate * gain[...]).astype(BF)
        normed_ref[...] = normed
        given = cotangent[...]
        added = []
        grad_normed = jnp.zeros_like(middle)
        for h in range(2):
            down = block(DOWN_AT + h * WIDTH)
            grad_act = dot_rows(given, down)
            for k in range(4):
                at = k * 512 + h * 256
                gate = dot(normed, weight[:, FFN_GATE_AT + at : FFN_GATE_AT + at + 256])
                up = dot(normed, weight[:, FFN_UP_AT + at : FFN_UP_AT + at + 256])
                share = 1.0 / (1.0 + jnp.exp(-gate))
                silu = gate * share
                act = (silu * up).astype(BF)
                act_ref[:, at : at + 256] = act
                grad = grad_act[:, k * 256 : (k + 1) * 256]
                mid_core[:, at : at + 256] = (
                    grad * up * share * (1.0 + gate * (1.0 - share))
                ).astype(BF)
                mid_core[:, 2048 + at : 2048 + at + 256] = (grad * silu).astype(BF)
            added.append(dot(half_of(act_ref, h), down))
        output[...] = (middle + (added[0] + added[1])).astype(BF)
        for j in range(4):
            at = j * WIDTH
            grad_normed = grad_normed + dot_rows(
                mid_core[:, at : at + WIDTH], block(FFN_GATE_AT + at)
            )
        grad_value, grad_gain[...] = norm_back(middle, rate, gain[...], grad_normed)
        grad_middle = given.astype(F32) + grad_value
        grad_middle_ref[...] = grad_middle
        branch = grad_middle.astype(BF)
        for h in range(2):
            grad = dot_rows(branch, block(OUT_AT + h * WIDTH))
            for k in range(4):
                at = k * MIX_SHARD + h * 256
                piece = grad[:, k * 256 : (k + 1) * 256]
                if h == 0:
                    grad_norm_ref[:, at : at + 256] = piece
                else:
                    grad_norm_ref[:, at : at + 128] = piece[:, :128]
                    grad_context_ref[:, k * 128 : (k + 1) * 128] = piece[:, 128:].astype(BF)
        mid_x[:, :4096] = mid_core[:, :4096]
        columns_for_others(shard, normed_ref, W_SHARD, mid_x, mid_core, 4096)
        rest_x[:, :WIDTH] = branch
        rest_core[:, :WIDTH] = branch
        columns_for_others(shard, act_ref, FF_SHARD, rest_x, rest_core, WIDTH)

    rows = tokens.shape[0]
    return call(
        body,
        [
            ((rows, WIDTH), BF),
            ((rows, WIDTH), BF),
            ((rows, 2048), BF),
            ((rows, WIDTH), F32),
            ((rows, DS), F32),
            ((rows, QW), BF),
            ((1, WIDTH), F32),
            ((rows, 4096 + 2 * W_SHARD), BF),
            ((rows, 4096 + W_SHARD), BF),
            ((rows, WIDTH + 2 * FF_SHARD), BF),
            ((rows, WIDTH + FF_SHARD), BF),
        ],
        [SMEM] + [VMEM] * 4 + [ANY] * PIECES,
        [pltpu.VMEM((WIDTH, REST_COLS), BF), pltpu.SemaphoreType.DMA((PIECES,))],
        "feed_forward",
        flops=4 * rows * WIDTH * REST_COLS,
        moved=2 * WIDTH * REST_COLS,
    )(meta, tokens, cotangent, side, gain, *pieces)


def exchange(to_x, to_core):
    far = over_x(to_x)
    return core(to_core), far, core(far)


def weight_products(meta, groups, name, cuts=(0,)):
    tokens = groups[0][3].shape[0]
    arrays = []

    def slot(array):
        for i, known in enumerate(arrays):
            if known is array:
                return i
        arrays.append(array)
        return len(arrays) - 1

    plan = [
        (
            width,
            w,
            [(slot(a), at) for a, at in grads],
            slot(own),
            [(slot(a), at) for a, at in others],
        )
        for width, w, grads, own, others in groups
    ]
    count, many = len(arrays), len(plan)
    pieces = [
        (i, at, end)
        for i, (width, *_) in enumerate(plan)
        for at, end in zip(cuts, cuts[1:] + (width,))
    ]

    def body(meta, *refs):
        sources, refs = refs[:count], refs[count:]
        outs, refs = refs[: len(pieces)], refs[len(pieces) :]
        lefts, rights, sems = refs[:many], refs[many : 2 * many], refs[2 * many]
        pairs = []
        for (width, w, grads, own, others), left, right in zip(plan, lefts, rights):
            at_own = pl.multiple_of(meta[0] * w, 128)
            columns = [(own, at_own)] + others
            for i in range(4):
                here = pl.ds(i * tokens, tokens)
                source, at = grads[i]
                pairs.append((sources[source].at[:, pl.ds(at, width)], right.at[here]))
                source, at = columns[i]
                pairs.append((sources[source].at[:, pl.ds(at, w)], left.at[here]))
        run_copies(pairs, sems)
        for out, (i, start, end) in zip(outs, pieces):
            turned, right = lefts[i][...], rights[i]
            for j in range(start, end, 256):
                step = min(256, end - j)
                out[:, j - start : j - start + step] = dot_tokens(
                    turned, right[:, j : j + step]
                ).astype(BF)

    return call(
        body,
        [((plan[i][1], end - start), BF) for i, start, end in pieces],
        [SMEM] + [ANY] * count,
        [pltpu.VMEM((4 * tokens, w), BF) for _, w, *_ in plan]
        + [pltpu.VMEM((4 * tokens, width), BF) for width, *_ in plan]
        + [pltpu.SemaphoreType.DMA((8 * many,))],
        name,
    )(meta, *arrays)


def bit_of(index, bit):
    return (index // bit) & 1


def halve(total, rep, bit):
    total = total.reshape(total.shape[0] // 2, 2, -1, total.shape[-1])
    mine = bit_of(rep, bit)
    return (
        lax.dynamic_index_in_dim(total, 1 - mine, 1, keepdims=False),
        lax.dynamic_index_in_dim(total, mine, 1, keepdims=False),
    )


def add(kept, arrived):
    return kept.astype(F32) + arrived.astype(F32)


def reduce_rep(total, sent, rep, *others):
    bit = 1
    while bit < lax.axis_size("rep"):
        half, kept = halve(total.astype(BF), rep, bit)
        arrived = swap(sent if bit == 1 else half, "rep", bit)
        if bit == 1 and others:
            arrived = after(arrived, *others)
        total = add(kept, arrived)
        bit *= 2
    return total.reshape(-1, total.shape[-1])


def reduce_small(blocks, shard, rep):
    total = blocks
    for axis, index, bit in (("shard", shard, 2), ("shard", shard, 1)):
        mine = bit_of(index, bit)
        total = total.reshape((2, -1) + blocks.shape[1:])
        arrived = swap(
            lax.dynamic_index_in_dim(total, 1 - mine, 0, keepdims=False), axis, bit
        )
        total = lax.dynamic_index_in_dim(total, mine, 0, keepdims=False) + arrived
    total = total.reshape(blocks.shape[1:])
    bit = lax.axis_size("rep") // 2
    while bit:
        mine = bit_of(rep, bit)
        total = total.reshape(2, -1, total.shape[-1])
        arrived = swap(
            lax.dynamic_index_in_dim(total, 1 - mine, 0, keepdims=False), "rep", bit
        )
        total = lax.dynamic_index_in_dim(total, mine, 0, keepdims=False) + arrived
        bit //= 2
    return total.reshape(-1)


def local(
    tokens,
    cotangent,
    first_gain,
    mixer_gate,
    mixer_input,
    step_weight,
    conv_weight,
    conv_bias,
    step_bias,
    decay_log,
    skip_weight,
    mixer_gain,
    mixer_output,
    query_matrix,
    key_matrix,
    value_matrix,
    attn_output,
    second_gain,
    ffn_gate,
    ffn_up,
    ffn_down,
):
    shard = lax.axis_index("shard")
    rep = lax.axis_index("rep")
    reps = lax.axis_size("rep")

    small_parts = (
        first_gain,
        conv_weight.reshape(-1),
        conv_bias,
        step_bias,
        decay_log,
        skip_weight,
        mixer_gain,
        second_gain,
    )
    small = jnp.concatenate(small_parts)
    small = jnp.pad(small, (0, -small.shape[0] % 128)).reshape(1, -1)
    far_small = over_x(small)
    smalls = jnp.concatenate([small, core(small), far_small, core(far_small)], axis=0)
    smalls = jnp.take(smalls, jnp.arange(4) ^ shard, axis=0).astype(F32)
    full, at = [], 0
    for part in small_parts:
        full.append(smalls[:, at : at + part.shape[0]])
        at += part.shape[0]
    taps = full[1].reshape(4, KC, -1).transpose(1, 0, 2).reshape(KC, XBC)
    gain_one, offset, step_offset, decay_rates, skip_scale, gain_mixer, gain_two = (
        full[i].reshape(-1) for i in (0, 2, 3, 4, 5, 6, 7)
    )

    meta = jnp.stack([shard, rep]).astype(jnp.int32)
    in_weights = (step_weight, mixer_gate, mixer_input, query_matrix, key_matrix, value_matrix)
    in_first = pack_in_quarter(meta, *in_weights)
    rest_packed, rest_first = pack_rest(
        meta, in_first, mixer_output, attn_output, ffn_gate, ffn_up, ffn_down
    )
    in_packed = pack_in(*in_weights)
    in_first = over_x(in_first)
    rest_first = over_x(after(rest_first, in_first, far_small))
    in_pieces = spread(in_packed, core(in_packed), in_first, rest_first)
    mixer_rows_of = DS // 4
    ff = 2048

    gain_one, gain_two = gain_one.reshape(1, -1), gain_two.reshape(1, -1)
    normalized_input, norm_x, norm_core, projected = project_in(
        meta, tokens, gain_one, in_pieces
    )
    rest_near = core(rest_packed)
    rest_parts = spread_first(rest_first, *in_pieces[5:7])
    def lanes(vector):
        return jnp.pad(vector, (0, 128 - HM)).reshape(1, 128)

    mixer_small = (
        taps,
        offset.reshape(1, -1),
        lanes(step_offset),
        lanes(decay_rates),
        jnp.repeat(skip_scale, P_SIZE).reshape(1, -1),
        gain_mixer.reshape(1, -1),
    )
    side, side_x, side_core = mix(meta, projected, *mixer_small)
    rest_pieces = spread_last(rest_packed, rest_near, rest_parts, normalized_input, side)
    (
        output,
        normed_two,
        activated,
        grad_middle,
        grad_mixer_norm,
        grad_context,
        grad_gain_two,
        mid_x,
        mid_core,
        rest_x,
        rest_core,
    ) = feed_forward(
        meta, tokens, cotangent, side, gain_two, rest_pieces
    )
    given = cotangent
    given_others = exchange(given, given)
    norm_others = exchange(norm_x, norm_core)
    side_others = exchange(side_x, side_core)
    early = (given_others[1], norm_others[1], side_others[1])
    mid_far = over_x(after(mid_x, *early))
    (
        in_own,
        grad_gain_mixer,
        grad_taps,
        grad_offset,
        grad_step_offset,
        grad_decay,
        grad_skip,
    ) = mix_back(projected, *mixer_small, grad_mixer_norm, grad_context)
    mid_far = after(mid_far, in_own)
    grad_step_offset, grad_decay = grad_step_offset[0, :HM], grad_decay[0, :HM]
    grad_skip = grad_skip.reshape(HM, P_SIZE).sum(axis=1)
    def at(arrays, *offsets):
        return list(zip(arrays, offsets))

    mid_others = (core(mid_core), mid_far, core(mid_far))
    in_far = over_x(in_own)
    (mid_blocks,) = weight_products(
        meta,
        [
            (
                4096,
                W_SHARD,
                at((mid_core,) + mid_others, 0, 0, 0, 0),
                normed_two,
                at(mid_others, 4096, 4096, 4096 + W_SHARD),
            )
        ],
        "mid_products",
    )
    mid_blocks = mid_blocks.reshape(reps, -1, 4096)
    mid_sent = halve(mid_blocks, rep, 1)[0]
    tokens_grad, grad_gain_one = project_in_back(
        meta, tokens, gain_one, in_own, after(grad_middle, mid_sent), in_pieces
    )
    in_far = after(in_far, tokens_grad)
    in_others = (core(in_own), in_far, core(in_far))
    rest_far = over_x(after(rest_x, in_far))
    in_cut = 2048
    in_low, in_high = weight_products(
        meta,
        [
            (
                IN_COLS,
                W_SHARD,
                at((in_own,) + in_others, 0, 0, 0, 0),
                normalized_input,
                at(norm_others, 0, 0, W_SHARD),
            )
        ],
        "in_products",
        (0, in_cut),
    )
    in_low, in_high = (blocks.reshape(reps, -1, blocks.shape[1]) for blocks in (in_low, in_high))
    in_low_sent, in_high_sent = (halve(blocks, rep, 1)[0] for blocks in (in_low, in_high))
    mid_grad = reduce_rep(mid_blocks, mid_sent, rep, in_low_sent)
    rest_far = after(rest_far, in_low_sent)
    rest_others = (core(rest_core), rest_far, core(rest_far))
    down_grad, out_grad = weight_products(
        meta,
        [
            (
                WIDTH,
                FF_SHARD,
                at((given,) + given_others, 0, 0, 0, 0),
                activated,
                at(rest_others, WIDTH, WIDTH, WIDTH + FF_SHARD),
            ),
            (
                WIDTH,
                OUT_SHARD,
                at((rest_core,) + rest_others, 0, 0, 0, 0),
                side,
                at(side_others, 0, 0, OUT_SHARD),
            ),
        ],
        "rest_products",
    )
    rest_blocks = jnp.concatenate(
        [
            down_grad.reshape(reps, -1, WIDTH),
            out_grad[:mixer_rows_of].reshape(reps, -1, WIDTH),
            out_grad[mixer_rows_of:].reshape(reps, -1, WIDTH),
        ],
        axis=1,
    )
    rest_sent = halve(rest_blocks, rep, 1)[0]
    in_grad = jnp.concatenate(
        [
            reduce_rep(in_low, in_low_sent, rep, rest_sent),
            reduce_rep(in_high, in_high_sent, rep, rest_sent),
        ],
        axis=1,
    )
    rest_grad = reduce_rep(rest_blocks, rest_sent, rep)
    down_m = FF_SHARD // reps
    down, out_grad = rest_grad[:down_m], rest_grad[down_m:]

    def blocks(vector):
        return vector.reshape(4, reps, -1)

    heads = jnp.concatenate(
        [grad_step_offset.reshape(4, -1), grad_decay.reshape(4, -1), grad_skip.reshape(4, -1)],
        axis=1,
    )
    small_grads = (
        blocks(grad_gain_one),
        grad_taps.reshape(KC, 4, reps, -1).transpose(1, 2, 0, 3).reshape(4, reps, -1),
        blocks(grad_offset),
        blocks(grad_gain_mixer),
        blocks(grad_gain_two),
        jnp.broadcast_to(heads[:, None, :], (4, reps, heads.shape[1])),
    )
    small_total = reduce_small(
        after(jnp.concatenate(small_grads, axis=2), rest_sent), shard, rep
    )
    smalls_out, at = [], 0
    for part in small_grads:
        smalls_out.append(small_total[at : at + part.shape[2]])
        at += part.shape[2]
    gain_one_out, taps_out, offset_out, gain_mixer_out, gain_two_out, heads_out = smalls_out
    each = HM // 4
    mixer_m = mixer_rows_of // reps
    return (
        output,
        tokens_grad,
        gain_one_out,
        in_grad[:, GATE_AT:MIXED_AT],
        in_grad[:, MIXED_AT:Q_AT],
        in_grad[:, STEP_AT : STEP_AT + HM],
        taps_out.reshape(KC, -1),
        offset_out,
        heads_out[:each],
        heads_out[each : 2 * each],
        heads_out[2 * each :],
        gain_mixer_out,
        out_grad[:mixer_m],
        in_grad[:, Q_AT:K_AT],
        in_grad[:, K_AT:V_AT],
        in_grad[:, V_AT:STEP_AT],
        out_grad[mixer_m:],
        gain_two_out,
        mid_grad[:, :ff],
        mid_grad[:, ff:],
        down,
    )


def solution(mesh):
    both = P(("shard", "rep"), None)
    rows, vector = P("shard", None), P("shard")
    owned = P(("shard", "rep"))
    return jax.shard_map(
        local,
        mesh=mesh,
        in_specs=(
            both,
            both,
            vector,
            rows,
            rows,
            rows,
            P(None, "shard"),
            vector,
            vector,
            vector,
            vector,
            vector,
            rows,
            rows,
            rows,
            rows,
            rows,
            vector,
            rows,
            rows,
            rows,
        ),
        out_specs=(
            both,
            both,
            owned,
            both,
            both,
            both,
            P(None, ("shard", "rep")),
            owned,
            vector,
            vector,
            vector,
            owned,
            both,
            both,
            both,
            both,
            both,
            owned,
            both,
            both,
            both,
        ),
        check_vma=False,
    )
```

```python
import jax
import jax.numpy as jnp
from jax import lax
from jax.experimental import pallas as pl
from jax.experimental.pallas import tpu as pltpu
from jax.sharding import PartitionSpec as P

QUERY_HEADS = 8
KEY_VALUE_HEADS = 2
HEAD_WIDTH = 64
HM = 24
P_SIZE = 64
N = 128
KC = 4
SEQUENCE_LENGTH = 128
DS = 1536
XBC = 1792
WIDTH = 1024
QW = QUERY_HEADS * HEAD_WIDTH
KW = KEY_VALUE_HEADS * HEAD_WIDTH
GATE_AT, MIXED_AT = 0, DS
Q_AT = MIXED_AT + XBC
K_AT = Q_AT + QW
V_AT = K_AT + KW
STEP_AT = V_AT + KW
IN_COLS = STEP_AT + 128


EPS = 1e-05
HIGH = lax.Precision.HIGHEST
BF = jnp.bfloat16
F32 = jnp.float32


def swap(value, axis, bit):
    size = lax.axis_size(axis)
    return lax.ppermute(value, axis, [(i, i ^ bit) for i in range(size)])


def core(value):
    return swap(value, "shard", 1)


def over_x(value):
    return swap(value, "shard", 2)


def over_y(value):
    return swap(value, "rep", 1)


def over_z(value):
    return swap(value, "rep", 2)


def over_zz(value):
    return swap(value, "rep", 4)


ANY = pl.BlockSpec(memory_space=pltpu.HBM)
VMEM = pl.BlockSpec(memory_space=pltpu.VMEM)
SMEM = pl.BlockSpec(memory_space=pltpu.SMEM)
VMEM_LIMIT = 60 << 20


def call(body, outs, in_specs, scratch, name, flops=0, moved=0):
    return pl.pallas_call(
        body,
        out_shape=[jax.ShapeDtypeStruct(shape, dtype) for shape, dtype in outs],
        in_specs=in_specs,
        out_specs=[VMEM] * len(outs),
        scratch_shapes=scratch,
        compiler_params=pltpu.CompilerParams(vmem_limit_bytes=VMEM_LIMIT),
        name=name,
        cost_estimate=pl.CostEstimate(flops=0, bytes_accessed=0, transcendentals=0),
    )


def run_copies(pairs, sems):
    copies = [
        pltpu.make_async_copy(source, target, sems.at[i]) for i, (source, target) in enumerate(pairs)
    ]
    for copy in copies:
        copy.start()
    for copy in copies:
        copy.wait()


def after(value, *others):
    def body(*refs):
        del refs

    return pl.pallas_call(
        body,
        out_shape=jax.ShapeDtypeStruct(value.shape, value.dtype),
        in_specs=[ANY] * (1 + len(others)),
        out_specs=ANY,
        input_output_aliases={0: 0},
        name="after",
    )(value, *others)


def dot(left, right):
    return jnp.dot(left, right, preferred_element_type=F32)


def dot_rows(left, right):
    return lax.dot_general(left, right, (((1,), (1,)), ((), ())), preferred_element_type=F32)


def dot_tokens(left, right):
    return lax.dot_general(left, right, (((0,), (0,)), ((), ())), preferred_element_type=F32)


def quarter(meta, rows):
    part = rows // 4
    return part, pl.multiple_of((meta[1] & 3) * part, part)


IN_PARTS = (
    (GATE_AT, DS),
    (MIXED_AT, XBC),
    (Q_AT, QW),
    (K_AT, KW),
    (V_AT, KW),
)


def pack_in_quarter(meta, step, mixer_gate, mixer_input, query, key, value):
    rows = step.shape[0]

    def body(meta, step, *refs):
        weights, (target, sems) = refs[:5], refs[5:]
        part, start = quarter(meta, rows)
        target[:, STEP_AT:] = jnp.zeros((part, IN_COLS - STEP_AT), BF)
        target[:, STEP_AT : STEP_AT + HM] = step[pl.ds(start, part), :]
        run_copies(
            [
                (weight.at[pl.ds(start, part)], target.at[:, pl.ds(at, width)])
                for (at, width), weight in zip(IN_PARTS, weights)
            ],
            sems,
        )

    return call(
        body,
        [((rows // 4, IN_COLS), BF)],
        [SMEM, VMEM] + [ANY] * 5,
        [pltpu.SemaphoreType.DMA((5,))],
        "pack_in_quarter",
    )(meta, step, mixer_gate, mixer_input, query, key, value)[0]


def pack_in(step, mixer_gate, mixer_input, query, key, value):
    rows = step.shape[0]

    def body(step, *refs):
        weights, (target, sems) = refs[:5], refs[5:]
        target[:, STEP_AT:] = jnp.zeros((rows, IN_COLS - STEP_AT), BF)
        target[:, STEP_AT : STEP_AT + HM] = step[...]
        run_copies(
            [
                (weight, target.at[:, pl.ds(at, width)])
                for (at, width), weight in zip(IN_PARTS, weights)
            ],
            sems,
        )

    return call(
        body,
        [((rows, IN_COLS), BF)],
        [VMEM] + [ANY] * 5,
        [pltpu.SemaphoreType.DMA((5,))],
        "pack_in",
        moved=4 * rows * IN_COLS,
    )(step, mixer_gate, mixer_input, query, key, value)[0]


OUT_AT, FFN_GATE_AT, FFN_UP_AT, DOWN_AT = 0, 2048, 4096, 6144
REST_COLS = 8192


def pack_rest(meta, behind, mixer_output, attn_output, gate, up, down):
    rows = gate.shape[0]
    half = rows // 2

    def body(meta, behind, mixer_output, attn_output, gate, up, down, target, first, sems):
        def block(at, width=WIDTH):
            return target.at[:, pl.ds(at, width)]

        low = target.at[pl.ds(0, half), pl.ds(OUT_AT + WIDTH, WIDTH)]
        high = target.at[pl.ds(half, half), pl.ds(OUT_AT + WIDTH, WIDTH)]
        pairs = [
            (mixer_output.at[pl.ds(0, rows)], block(OUT_AT)),
            (gate, block(FFN_GATE_AT, 2048)),
            (up, block(FFN_UP_AT, 2048)),
            (down.at[pl.ds(0, rows)], block(DOWN_AT)),
            (down.at[pl.ds(rows, rows)], block(DOWN_AT + WIDTH)),
            (mixer_output.at[pl.ds(rows, half)], low),
            (attn_output, high),
        ]
        run_copies(pairs, sems)
        part, start = quarter(meta, rows)
        first[...] = target[pl.ds(start, part), :]

    return call(
        body,
        [((rows, REST_COLS), BF), ((rows // 4, REST_COLS), BF)],
        [SMEM] + [ANY] * 6,
        [pltpu.SemaphoreType.DMA((7,))],
        "pack_rest",
    )(meta, behind, mixer_output, attn_output, gate, up, down)


def spread(packed, near, first, last):
    half = first.shape[0] // 2
    from_y, from_z = over_y(first), over_z(first)
    low, high = over_y(from_z[:half]), over_z(from_y[half:])
    far = (first, from_y, from_z, after(low, last), after(high, last))
    return (packed, near) + far + tuple(core(piece) for piece in far)


def spread_first(first, *others):
    first = after(first, *others)
    return first, over_y(first), over_z(first)


def spread_last(packed, near, parts, middle, end):
    first, from_y, from_z = parts
    half = first.shape[0] // 2
    from_y, from_z = after(from_y, middle), after(from_z, middle)
    low, high = over_y(from_z[:half]), over_z(from_y[half:])
    far = (first, from_y, from_z, low, high)
    others = tuple(core(piece) for piece in far[:3])
    low, high = after(low, end), after(high, end)
    return (packed, near, first, from_y, from_z, low, high) + others + (core(low), core(high))


def fill(meta, pieces, target, sems):
    shard, mine = meta[0], meta[1] & 3
    rows = pieces[0].shape[0]
    part = rows // 4
    pairs = [
        (pieces[0], target.at[pl.ds(pl.multiple_of(shard * rows, rows), rows)]),
        (pieces[1], target.at[pl.ds(pl.multiple_of((shard ^ 1) * rows, rows), rows)]),
    ]
    for at, owner in ((2, shard ^ 2), (7, shard ^ 3)):
        for j, add in enumerate((0, 0, 0, 0, part // 2)):
            start = pl.multiple_of(owner * rows + (mine ^ min(j, 3)) * part + add, part // 2)
            size = part if j < 3 else part // 2
            pairs.append((pieces[at + j], target.at[pl.ds(start, size)]))
    run_copies(pairs, sems)


PIECES = 12
MIX_SHARD, ATT_SHARD, FF_SHARD, W_SHARD = DS // 4, QW // 4, 512, WIDTH // 4
OUT_SHARD = MIX_SHARD + ATT_SHARD


def columns_of(ref, shard, width):
    return ref[:, pl.ds(pl.multiple_of(shard * width, 128), width)]


NORM_AT = 4096 + WIDTH
ACT_AT_X, ACT_AT_CORE = NORM_AT + 2 * W_SHARD, NORM_AT + W_SHARD


def columns_for_others(shard, ref, width, to_x, to_core, at=0, at_core=0):
    to_x[:, at : at + width] = columns_of(ref, shard ^ 2, width)
    to_x[:, at + width : at + 2 * width] = columns_of(ref, shard ^ 3, width)
    to_core[:, at_core : at_core + width] = columns_of(ref, shard ^ 1, width)


def norm_rate(value):
    return lax.rsqrt(jnp.mean(value * value, axis=-1, keepdims=True) + EPS)


def norm_back(value, rate, gain, grad):
    scaled = gain * grad
    grad_value = rate * scaled - value * (rate * rate * rate) * jnp.mean(
        value * scaled, axis=-1, keepdims=True
    )
    return grad_value, jnp.sum(value * rate * grad, axis=0, keepdims=True)


def project_in(meta, tokens, gain, pieces):
    def body(meta, tokens, gain, *refs):
        pieces, (normed_ref, to_x, to_core, out, weight, sems) = refs[:PIECES], refs[PIECES:]
        fill(meta, pieces, weight, sems)
        value = tokens[...].astype(F32)
        normed = (value * norm_rate(value) * gain[...]).astype(BF)
        normed_ref[...] = normed
        columns_for_others(meta[0], normed_ref, W_SHARD, to_x, to_core)
        out[...] = dot(normed, weight[...])

    rows = tokens.shape[0]
    return call(
        body,
        [
            ((rows, WIDTH), BF),
            ((rows, 2 * W_SHARD), BF),
            ((rows, W_SHARD), BF),
            ((rows, IN_COLS), F32),
        ],
        [SMEM, VMEM, VMEM] + [ANY] * PIECES,
        [pltpu.VMEM((WIDTH, IN_COLS), BF), pltpu.SemaphoreType.DMA((PIECES,))],
        "project_in",
        flops=2 * rows * WIDTH * IN_COLS,
        moved=2 * WIDTH * IN_COLS,
    )(meta, tokens, gain, *pieces)


def project_in_back(meta, tokens, gain, grad_projected, grad_middle, pieces):
    def body(meta, tokens, gain, grad_projected, grad_middle, *refs):
        pieces, (out, grad_gain, weight, sems) = refs[:PIECES], refs[PIECES:]
        fill(meta, pieces, weight, sems)
        value = tokens[...].astype(F32)
        rate = norm_rate(value)
        grad = dot_rows(grad_projected[:, :IN_COLS], weight[...])
        grad_value, grad_gain[...] = norm_back(value, rate, gain[...], grad)
        out[...] = (grad_middle[...] + grad_value).astype(BF)

    rows = tokens.shape[0]
    return call(
        body,
        [((rows, WIDTH), BF), ((1, WIDTH), F32)],
        [SMEM] + [VMEM] * 4 + [ANY] * PIECES,
        [pltpu.VMEM((WIDTH, IN_COLS), BF), pltpu.SemaphoreType.DMA((PIECES,))],
        "project_in_back",
        flops=2 * rows * WIDTH * IN_COLS,
        moved=2 * WIDTH * IN_COLS,
    )(meta, tokens, gain, grad_projected, grad_middle, *pieces)


def silu_parts(value):
    share = 1.0 / (1.0 + jnp.exp(-value))
    return value * share, share


def silu_slope(value, share):
    return share * (1.0 + value * (1.0 - share))


def exact(left, right, axes=((1,), (0,))):
    return lax.dot_general(
        left, right, (axes, ((), ())), precision=HIGH, preferred_element_type=F32
    )


def causal_mask(rows):
    return lax.broadcasted_iota(jnp.int32, (rows, rows), 0) >= lax.broadcasted_iota(
        jnp.int32, (rows, rows), 1
    )


EDGE = 8


def mixer_state(projected, taps, offset, step_offset, decay, padded, causal):
    rows = projected.shape[0]
    padded[:EDGE] = jnp.zeros((EDGE, XBC), F32)
    padded[EDGE:] = projected[:, MIXED_AT:Q_AT]
    convolved = offset[...]
    for o in range(KC):
        start = EDGE - KC + 1 + o
        convolved = convolved + padded[start : start + rows] * taps[o : o + 1]
    active, share = silu_parts(convolved)
    raw = projected[:, STEP_AT:] + step_offset[...]
    step = jnp.maximum(raw, 0.0) + jnp.log1p(jnp.exp(-jnp.abs(raw)))
    rate = jnp.exp(decay[...])
    log_decay = -step * rate
    running = exact(causal.astype(F32), log_decay)
    return convolved, active, share, raw, step, rate, log_decay, running


def decay_of(running, running_t, causal, h):
    spread = running[:, h : h + 1] - running_t[h : h + 1]
    return jnp.where(causal, jnp.exp(jnp.where(causal, spread, 0.0)), 0.0)


def head(value, h):
    return value[:, h * HEAD_WIDTH : (h + 1) * HEAD_WIDTH]


def shares_of(query, key, causal):
    scores = jnp.where(causal, dot_rows(query, key) * HEAD_WIDTH ** (-0.5), -1e30)
    unscaled = jnp.exp(scores - jnp.max(scores, axis=-1, keepdims=True))
    return unscaled / jnp.sum(unscaled, axis=-1, keepdims=True)


def mix(meta, projected, taps, offset, step_offset, decay, skip, gain):
    rows = projected.shape[0]

    def body(meta, projected, taps, offset, step_offset, decay, skip, gain, *refs):
        side, to_x, to_core, result_ref, padded, active_ref = refs
        causal = causal_mask(rows)
        _, active, _, _, step, _, _, running = mixer_state(
            projected, taps, offset, step_offset, decay, padded, causal
        )
        active_ref[...] = active
        running_t, step_t = running.T, step.T
        coupling = exact(active[:, DS + N :], active[:, DS : DS + N], ((1,), (1,)))
        for h in range(HM):
            mixing = coupling * decay_of(running, running_t, causal, h) * step_t[h : h + 1]
            at = h * P_SIZE
            result_ref[:, at : at + P_SIZE] = exact(mixing, active_ref[:, at : at + P_SIZE])
        result = result_ref[...] + skip[...] * active_ref[:, :DS]
        gated = result * silu_parts(projected[:, GATE_AT:MIXED_AT])[0]
        mixed = (gated * norm_rate(gated) * gain[...]).astype(BF)
        for k in range(4):
            side[:, k * OUT_SHARD : k * OUT_SHARD + MIX_SHARD] = mixed[
                :, k * MIX_SHARD : (k + 1) * MIX_SHARD
            ]
        for h in range(QUERY_HEADS):
            query = projected[:, Q_AT + h * HEAD_WIDTH : Q_AT + (h + 1) * HEAD_WIDTH]
            at = (h // (QUERY_HEADS // KEY_VALUE_HEADS)) * HEAD_WIDTH
            key = projected[:, K_AT + at : K_AT + at + HEAD_WIDTH]
            value = projected[:, V_AT + at : V_AT + at + HEAD_WIDTH]
            shares = shares_of(query.astype(BF), key.astype(BF), causal)
            at = (h // 2) * OUT_SHARD + MIX_SHARD + (h % 2) * HEAD_WIDTH
            side[:, at : at + HEAD_WIDTH] = dot(shares.astype(BF), value.astype(BF)).astype(BF)
        columns_for_others(meta[0], side, OUT_SHARD, to_x, to_core)

    return call(
        body,
        [((rows, 4 * OUT_SHARD), BF), ((rows, 2 * OUT_SHARD), BF), ((rows, OUT_SHARD), BF)],
        [SMEM] + [VMEM] * 7,
        [
            pltpu.VMEM((rows, DS), F32),
            pltpu.VMEM((EDGE + rows, XBC), F32),
            pltpu.VMEM((rows, XBC), F32),
        ],
        "mix",
    )(meta, projected, taps, offset, step_offset, decay, skip, gain)


def mix_back(projected, taps, offset, step_offset, decay, skip, gain, grad_norm, grad_ctx):
    rows = projected.shape[0]

    def body(projected, taps, offset, step_offset, decay, skip, gain, grad_norm, grad_ctx, *refs):
        (
            to_core,
            grad_gain,
            grad_taps,
            grad_offset,
            grad_step_offset,
            grad_decay,
            grad_skip,
            result_ref,
            padded,
            active_ref,
            grad_active,
            column_ref,
            row_ref,
        ) = refs
        causal = causal_mask(rows)
        convolved, active, share, raw, step, rate, log_decay, running = mixer_state(
            projected, taps, offset, step_offset, decay, padded, causal
        )
        active_ref[...] = active
        running_t, step_t = running.T, step.T
        in_state, out_state = active[:, DS : DS + N], active[:, DS + N :]
        coupling = exact(out_state, in_state, ((1,), (1,)))
        for h in range(HM):
            mixing = coupling * decay_of(running, running_t, causal, h) * step_t[h : h + 1]
            at = h * P_SIZE
            result_ref[:, at : at + P_SIZE] = exact(mixing, active_ref[:, at : at + P_SIZE])
        inner = active_ref[:, :DS]
        result = result_ref[...] + skip[...] * inner
        gate = projected[:, GATE_AT:MIXED_AT]
        silu, gate_share = silu_parts(gate)
        gated = result * silu
        grad_gated, grad_gain[...] = norm_back(gated, norm_rate(gated), gain[...], grad_norm[...])
        to_core[:, GATE_AT:MIXED_AT] = (
            grad_gated * result * silu_slope(gate, gate_share)
        ).astype(BF)
        grad_result = grad_gated * silu
        result_ref[...] = grad_result
        grad_skip[...] = jnp.sum(grad_result * inner, axis=0, keepdims=True)
        grad_coupling = jnp.zeros((rows, rows), F32)
        column_ref[...] = jnp.zeros_like(column_ref)
        row_ref[...] = jnp.zeros_like(row_ref)
        for h in range(HM):
            at = h * P_SIZE
            decays = decay_of(running, running_t, causal, h)
            step_row = step_t[h : h + 1]
            scaled = decays * step_row
            grad_out = result_ref[:, at : at + P_SIZE]
            grad_active[:, at : at + P_SIZE] = exact(coupling * scaled, grad_out, ((0,), (0,)))
            grad_mixing = exact(grad_out, active_ref[:, at : at + P_SIZE], ((1,), (1,)))
            grad_coupling = grad_coupling + grad_mixing * scaled
            weighed = grad_mixing * decays * coupling
            row_ref[h : h + 1] = jnp.sum(weighed, axis=0, keepdims=True)
            column_ref[:, h : h + 1] = jnp.sum(weighed * step_row, axis=1, keepdims=True)
        grad_active[:, :DS] = grad_active[:, :DS] + skip[...] * result_ref[...]
        grad_active[:, DS : DS + N] = exact(grad_coupling, out_state, ((0,), (0,)))
        grad_active[:, DS + N :] = exact(grad_coupling, in_state)
        grad_step = row_ref[...].T
        grad_running = column_ref[...] - grad_step * step
        grad_log = exact(causal.astype(F32), grad_running, ((0,), (0,)))
        grad_decay[...] = jnp.sum(grad_log * log_decay, axis=0, keepdims=True)
        grad_raw = (grad_step - grad_log * rate) / (1.0 + jnp.exp(-raw))
        grad_step_offset[...] = jnp.sum(grad_raw, axis=0, keepdims=True)
        lanes = lax.broadcasted_iota(jnp.int32, (rows, 128), 1)
        to_core[:, STEP_AT:IN_COLS] = jnp.where(lanes < HM, grad_raw, 0.0).astype(BF)
        grad_conv = grad_active[...] * silu_slope(convolved, share)
        grad_offset[...] = jnp.sum(grad_conv, axis=0, keepdims=True)
        for o in range(KC):
            start = EDGE - KC + 1 + o
            grad_taps[o : o + 1] = jnp.sum(
                grad_conv * padded[start : start + rows], axis=0, keepdims=True
            )
        padded[:rows] = grad_conv
        padded[rows:] = jnp.zeros((EDGE, XBC), F32)
        grad_mixed = grad_conv * taps[KC - 1 : KC]
        for o in range(KC - 1):
            start = KC - 1 - o
            grad_mixed = grad_mixed + padded[start : start + rows] * taps[o : o + 1]
        to_core[:, MIXED_AT:Q_AT] = grad_mixed.astype(BF)

        group = QUERY_HEADS // KEY_VALUE_HEADS
        for kv in range(KEY_VALUE_HEADS):
            at = kv * HEAD_WIDTH
            key = projected[:, K_AT + at : K_AT + at + HEAD_WIDTH].astype(BF)
            value = projected[:, V_AT + at : V_AT + at + HEAD_WIDTH].astype(BF)
            grad_key = jnp.zeros((rows, HEAD_WIDTH), F32)
            grad_value = jnp.zeros((rows, HEAD_WIDTH), F32)
            for h in range(kv * group, (kv + 1) * group):
                query = projected[:, Q_AT + h * HEAD_WIDTH : Q_AT + (h + 1) * HEAD_WIDTH]
                query = query.astype(BF)
                shares = shares_of(query, key, causal)
                given = grad_ctx[:, h * HEAD_WIDTH : (h + 1) * HEAD_WIDTH]
                grad_shares = dot_rows(given, value)
                grad_value = grad_value + dot_tokens(shares.astype(BF), given)
                weighed = shares * grad_shares
                grad_scores = weighed - shares * jnp.sum(weighed, axis=-1, keepdims=True)
                grad_scores = (grad_scores * HEAD_WIDTH ** (-0.5)).astype(BF)
                to_core[:, Q_AT + h * HEAD_WIDTH : Q_AT + (h + 1) * HEAD_WIDTH] = dot(
                    grad_scores, key
                ).astype(BF)
                grad_key = grad_key + dot_tokens(grad_scores, query)
            to_core[:, K_AT + at : K_AT + at + HEAD_WIDTH] = grad_key.astype(BF)
            to_core[:, V_AT + at : V_AT + at + HEAD_WIDTH] = grad_value.astype(BF)
    return call(
        body,
        [
            ((rows, IN_COLS), BF),
            ((1, DS), F32),
            ((KC, XBC), F32),
            ((1, XBC), F32),
            ((1, 128), F32),
            ((1, 128), F32),
            ((1, DS), F32),
        ],
        [VMEM] * 9,
        [
            pltpu.VMEM((rows, DS), F32),
            pltpu.VMEM((EDGE + rows, XBC), F32),
            pltpu.VMEM((rows, XBC), F32),
            pltpu.VMEM((rows, XBC), F32),
            pltpu.VMEM((rows, 128), F32),
            pltpu.VMEM((128, rows), F32),
        ],
        "mix_back",
    )(projected, taps, offset, step_offset, decay, skip, gain, grad_norm, grad_ctx)


def feed_forward(meta, tokens, cotangent, side, gain, pieces):
    def body(meta, tokens, cotangent, side, gain, *refs):
        pieces, refs = refs[:PIECES], refs[PIECES:]
        (
            output,
            normed_ref,
            act_ref,
            grad_middle_ref,
            grad_norm_ref,
            grad_context_ref,
            grad_gain,
            to_x,
            mid_core,
            weight,
            sems,
        ) = refs
        fill(meta, pieces, weight, sems)
        shard = meta[0]

        def block(at):
            return weight[:, at : at + WIDTH]

        def half_of(ref, h):
            return jnp.concatenate(
                [ref[:, k * 512 + h * 256 : k * 512 + h * 256 + 256] for k in range(4)], axis=1
            )

        middle = tokens[...].astype(F32)
        for h in range(2):
            middle = middle + dot(half_of(side, h), block(OUT_AT + h * WIDTH))
        rate = norm_rate(middle)
        normed = (middle * rate * gain[...]).astype(BF)
        normed_ref[...] = normed
        given = cotangent[...]
        added = []
        grad_normed = jnp.zeros_like(middle)
        for h in range(2):
            down = block(DOWN_AT + h * WIDTH)
            grad_act = dot_rows(given, down)
            for k in range(4):
                at = k * 512 + h * 256
                gate = dot(normed, weight[:, FFN_GATE_AT + at : FFN_GATE_AT + at + 256])
                up = dot(normed, weight[:, FFN_UP_AT + at : FFN_UP_AT + at + 256])
                share = 1.0 / (1.0 + jnp.exp(-gate))
                silu = gate * share
                act = (silu * up).astype(BF)
                act_ref[:, at : at + 256] = act
                grad = grad_act[:, k * 256 : (k + 1) * 256]
                mid_core[:, at : at + 256] = (
                    grad * up * share * (1.0 + gate * (1.0 - share))
                ).astype(BF)
                mid_core[:, 2048 + at : 2048 + at + 256] = (grad * silu).astype(BF)
            added.append(dot(half_of(act_ref, h), down))
        output[...] = (middle + (added[0] + added[1])).astype(BF)
        for j in range(4):
            at = j * WIDTH
            grad_normed = grad_normed + dot_rows(
                mid_core[:, at : at + WIDTH], block(FFN_GATE_AT + at)
            )
        grad_value, grad_gain[...] = norm_back(middle, rate, gain[...], grad_normed)
        grad_middle = given.astype(F32) + grad_value
        grad_middle_ref[...] = grad_middle
        branch = grad_middle.astype(BF)
        for h in range(2):
            grad = dot_rows(branch, block(OUT_AT + h * WIDTH))
            for k in range(4):
                at = k * MIX_SHARD + h * 256
                piece = grad[:, k * 256 : (k + 1) * 256]
                if h == 0:
                    grad_norm_ref[:, at : at + 256] = piece
                else:
                    grad_norm_ref[:, at : at + 128] = piece[:, :128]
                    grad_context_ref[:, k * 128 : (k + 1) * 128] = piece[:, 128:].astype(BF)
        mid_core[:, 4096 : 4096 + WIDTH] = branch
        to_x[:, : 4096 + WIDTH] = mid_core[:, : 4096 + WIDTH]
        columns_for_others(shard, normed_ref, W_SHARD, to_x, mid_core, NORM_AT, NORM_AT)
        columns_for_others(shard, act_ref, FF_SHARD, to_x, mid_core, ACT_AT_X, ACT_AT_CORE)

    rows = tokens.shape[0]
    return call(
        body,
        [
            ((rows, WIDTH), BF),
            ((rows, WIDTH), BF),
            ((rows, 2048), BF),
            ((rows, WIDTH), F32),
            ((rows, DS), F32),
            ((rows, QW), BF),
            ((1, WIDTH), F32),
            ((rows, ACT_AT_X + 2 * FF_SHARD), BF),
            ((rows, ACT_AT_CORE + FF_SHARD), BF),
        ],
        [SMEM] + [VMEM] * 4 + [ANY] * PIECES,
        [pltpu.VMEM((WIDTH, REST_COLS), BF), pltpu.SemaphoreType.DMA((PIECES,))],
        "feed_forward",
        flops=4 * rows * WIDTH * REST_COLS,
        moved=2 * WIDTH * REST_COLS,
    )(meta, tokens, cotangent, side, gain, *pieces)


def exchange(to_x, to_core):
    far = over_x(to_x)
    return core(to_core), far, core(far)


def weight_products(meta, groups, name, cuts=(0,)):
    tokens = groups[0][3].shape[0]
    arrays = []

    def slot(array):
        for i, known in enumerate(arrays):
            if known is array:
                return i
        arrays.append(array)
        return len(arrays) - 1

    plan = [
        (
            width,
            w,
            [(slot(a), at) for a, at in grads],
            slot(own),
            [(slot(a), at) for a, at in others],
        )
        for width, w, grads, own, others in groups
    ]
    count, many = len(arrays), len(plan)
    pieces = [
        (i, at, end)
        for i, (width, *_) in enumerate(plan)
        for at, end in zip(cuts, cuts[1:] + (width,))
    ]

    def body(meta, *refs):
        sources, refs = refs[:count], refs[count:]
        outs, refs = refs[: len(pieces)], refs[len(pieces) :]
        lefts, rights, sems = refs[:many], refs[many : 2 * many], refs[2 * many]
        pairs = []
        for (width, w, grads, own, others), left, right in zip(plan, lefts, rights):
            at_own = pl.multiple_of(meta[0] * w, 128)
            columns = [(own, at_own)] + others
            for i in range(4):
                here = pl.ds(i * tokens, tokens)
                source, at = grads[i]
                pairs.append((sources[source].at[:, pl.ds(at, width)], right.at[here]))
                source, at = columns[i]
                pairs.append((sources[source].at[:, pl.ds(at, w)], left.at[here]))
        run_copies(pairs, sems)
        for out, (i, start, end) in zip(outs, pieces):
            turned, right = lefts[i][...], rights[i]
            for j in range(start, end, 256):
                step = min(256, end - j)
                out[:, j - start : j - start + step] = dot_tokens(
                    turned, right[:, j : j + step]
                ).astype(BF)

    return call(
        body,
        [((plan[i][1], end - start), BF) for i, start, end in pieces],
        [SMEM] + [ANY] * count,
        [pltpu.VMEM((4 * tokens, w), BF) for _, w, *_ in plan]
        + [pltpu.VMEM((4 * tokens, width), BF) for width, *_ in plan]
        + [pltpu.SemaphoreType.DMA((8 * many,))],
        name,
    )(meta, *arrays)


def bit_of(index, bit):
    return (index // bit) & 1


def halve(total, rep, bit, below=1):
    split = total.reshape((total.shape[0] // (2 * below), 2, below) + total.shape[1:])
    mine = bit_of(rep, bit)
    return tuple(
        lax.dynamic_index_in_dim(split, j, 1, keepdims=False).reshape((-1,) + total.shape[1:])
        for j in (1 - mine, mine)
    )


def add(kept, arrived):
    return kept.astype(F32) + arrived.astype(F32)


def step(total, rep, bit, below=1):
    sent, kept = halve(total, rep, bit, below)
    return sent, kept, swap(sent, "rep", bit)


def next_step(kept, arrived, rep, bit):
    return step(add(kept, arrived).astype(BF), rep, bit)


def last_steps(kept, arrived, rep, bit=8):
    total, held = add(kept, arrived), kept.dtype
    while bit < lax.axis_size("rep"):
        total = add(*step(total.astype(held), rep, bit)[1:])
        bit *= 2
    return total.reshape(-1, total.shape[-1])


def pick_bit(blocks, axis, bit):
    return tuple(
        lax.dynamic_index_in_dim(blocks, j, axis, keepdims=False) for j in (1 - bit, bit)
    )


def local(
    tokens,
    cotangent,
    first_gain,
    mixer_gate,
    mixer_input,
    step_weight,
    conv_weight,
    conv_bias,
    step_bias,
    decay_log,
    skip_weight,
    mixer_gain,
    mixer_output,
    query_matrix,
    key_matrix,
    value_matrix,
    attn_output,
    second_gain,
    ffn_gate,
    ffn_up,
    ffn_down,
):
    shard = lax.axis_index("shard")
    rep = lax.axis_index("rep")
    reps = lax.axis_size("rep")

    small_parts = (
        first_gain,
        conv_weight.reshape(-1),
        conv_bias,
        step_bias,
        decay_log,
        skip_weight,
        mixer_gain,
        second_gain,
    )
    small = jnp.concatenate(small_parts)
    small = jnp.pad(small, (0, -small.shape[0] % 128)).reshape(1, -1)
    far_small = over_x(small)
    smalls = jnp.concatenate([small, core(small), far_small, core(far_small)], axis=0)
    smalls = jnp.take(smalls, jnp.arange(4) ^ shard, axis=0).astype(F32)
    full, at = [], 0
    for part in small_parts:
        full.append(smalls[:, at : at + part.shape[0]])
        at += part.shape[0]
    taps = full[1].reshape(4, KC, -1).transpose(1, 0, 2).reshape(KC, XBC)
    gain_one, offset, step_offset, decay_rates, skip_scale, gain_mixer, gain_two = (
        full[i].reshape(-1) for i in (0, 2, 3, 4, 5, 6, 7)
    )

    meta = jnp.stack([shard, rep]).astype(jnp.int32)
    in_weights = (step_weight, mixer_gate, mixer_input, query_matrix, key_matrix, value_matrix)
    in_first = pack_in_quarter(meta, *in_weights)
    rest_packed, rest_first = pack_rest(
        meta, in_first, mixer_output, attn_output, ffn_gate, ffn_up, ffn_down
    )
    in_packed = pack_in(*in_weights)
    in_first = over_x(in_first)
    rest_first = over_x(after(rest_first, in_first, far_small))
    in_pieces = spread(in_packed, core(in_packed), in_first, rest_first)
    mixer_rows_of = DS // 4
    ff = 2048

    gain_one, gain_two = gain_one.reshape(1, -1), gain_two.reshape(1, -1)
    normalized_input, norm_x, norm_core, projected = project_in(
        meta, tokens, gain_one, in_pieces
    )
    rest_near = core(rest_packed)
    rest_parts = spread_first(rest_first, *in_pieces[5:7])
    def lanes(vector):
        return jnp.pad(vector, (0, 128 - HM)).reshape(1, 128)

    mixer_small = (
        taps,
        offset.reshape(1, -1),
        lanes(step_offset),
        lanes(decay_rates),
        jnp.repeat(skip_scale, P_SIZE).reshape(1, -1),
        gain_mixer.reshape(1, -1),
    )
    side, side_x, side_core = mix(meta, projected, *mixer_small)
    rest_pieces = spread_last(rest_packed, rest_near, rest_parts, normalized_input, side)
    (
        output,
        normed_two,
        activated,
        grad_middle,
        grad_mixer_norm,
        grad_context,
        grad_gain_two,
        mid_x,
        mid_core,
    ) = feed_forward(
        meta, tokens, cotangent, side, gain_two, rest_pieces
    )
    given = cotangent
    given_others = exchange(given, given)
    norm_others = exchange(norm_x, norm_core)
    side_others = exchange(side_x, side_core)
    early = (given_others[1], norm_others[1], side_others[1])
    mid_far = over_x(after(mid_x, *early))
    (
        in_own,
        grad_gain_mixer,
        grad_taps,
        grad_offset,
        grad_step_offset,
        grad_decay,
        grad_skip,
    ) = mix_back(projected, *mixer_small, grad_mixer_norm, grad_context)
    tokens_grad, grad_gain_one = project_in_back(
        meta, tokens, gain_one, in_own, grad_middle, in_pieces
    )
    mid_far = after(mid_far, in_own, tokens_grad)
    grad_step_offset, grad_decay = grad_step_offset[0, :HM], grad_decay[0, :HM]
    grad_skip = grad_skip.reshape(HM, P_SIZE).sum(axis=1)
    def blocks(vector):
        return vector.reshape(4, reps, -1)

    heads = jnp.concatenate(
        [grad_step_offset.reshape(4, -1), grad_decay.reshape(4, -1), grad_skip.reshape(4, -1)],
        axis=1,
    )
    small_grads = (
        blocks(grad_gain_one),
        grad_taps.reshape(KC, 4, reps, -1).transpose(1, 2, 0, 3).reshape(4, reps, -1),
        blocks(grad_offset),
        blocks(grad_gain_mixer),
        blocks(grad_gain_two),
        jnp.broadcast_to(heads[:, None, :], (4, reps, heads.shape[1])),
    )
    small = jnp.concatenate(small_grads, axis=2)
    small = small.reshape((2, 2) + small.shape[1:])
    sent, small_kept = pick_bit(small, 1, bit_of(shard, 1))
    small_core = core(sent)

    def at(arrays, *offsets):
        return list(zip(arrays, offsets))

    mid_others = (core(mid_core), mid_far, core(mid_far))
    in_far = over_x(in_own)
    mid_all = (mid_core,) + mid_others
    mid_low, mid_high = weight_products(
        meta,
        [
            (
                4096,
                W_SHARD,
                at(mid_all, 0, 0, 0, 0),
                normed_two,
                at(mid_others, NORM_AT, NORM_AT, NORM_AT + W_SHARD),
            )
        ],
        "mid_products",
        (0, 2048),
    )
    low_sent, low_kept, low_y = step(mid_low.reshape(reps, -1, 2048), rep, 1)
    high_sent, high_kept, high_z = step(mid_high.reshape(reps, -1, 2048), rep, 2, 2)
    down_blocks, out_blocks = weight_products(
        meta,
        [
            (
                WIDTH,
                FF_SHARD,
                at((given,) + given_others, 0, 0, 0, 0),
                activated,
                at(mid_others, ACT_AT_CORE, ACT_AT_X, ACT_AT_X + FF_SHARD),
            ),
            (
                WIDTH,
                OUT_SHARD,
                at(mid_all, 4096, 4096, 4096, 4096),
                side,
                at(side_others, 0, 0, OUT_SHARD),
            ),
        ],
        "rest_products",
    )
    out_blocks = jnp.concatenate(
        [
            out_blocks[:mixer_rows_of].reshape(reps, -1, WIDTH),
            out_blocks[mixer_rows_of:].reshape(reps, -1, WIDTH),
        ],
        axis=1,
    )
    down_sent, down_kept, down_y = step(down_blocks.reshape(reps, -1, WIDTH), rep, 1)
    out_sent, out_kept, out_z = step(out_blocks, rep, 2, 2)

    low_y = after(low_y, high_z, small_core)
    in_far = after(in_far, low_y, down_sent, out_sent)
    _, low_kept, low_z = next_step(low_kept, low_y, rep, 2)
    _, high_kept, high_y = next_step(high_kept, high_z, rep, 1)
    small_core = after(small_core, in_far)
    sent, small_kept = pick_bit(small_kept + small_core, 0, bit_of(shard, 2))
    small_x = over_x(sent)
    in_others = (core(in_own), in_far, core(in_far))
    in_cut = 2048
    in_low, in_high = weight_products(
        meta,
        [
            (
                IN_COLS,
                W_SHARD,
                at((in_own,) + in_others, 0, 0, 0, 0),
                normalized_input,
                at(norm_others, 0, 0, W_SHARD),
            )
        ],
        "in_products",
        (0, in_cut),
    )
    a_sent, a_kept, a_y = step(in_low.reshape(reps, -1, in_cut), rep, 1)
    b_sent, b_kept, b_y = step(in_high.reshape(reps, -1, IN_COLS - in_cut), rep, 1)

    down_y, out_z = after(down_y, a_sent, b_sent), after(out_z, a_sent, b_sent)
    low_z, high_y = after(low_z, a_sent, b_sent), after(high_y, a_sent, b_sent)
    small_x = after(small_x, a_sent, b_sent)
    down_sent, down_kept, down_z = next_step(down_kept, down_y, rep, 2)
    out_sent, out_kept, out_y = next_step(out_kept, out_z, rep, 1)
    low_sent, low_kept, low_zz = next_step(low_kept, low_z, rep, 4)
    high_sent, high_kept, high_zz = next_step(high_kept, high_y, rep, 4)
    _, small_kept, small_z = step((small_kept + small_x)[:, None], rep, 2, 2)

    a_y = after(a_y, down_sent, out_sent, low_sent, high_sent)
    a_sent, a_kept, a_z = next_step(a_kept, a_y, rep, 2)
    down_z, out_y, small_z = after(down_z, a_sent), after(out_y, a_sent), after(small_z, a_sent)
    down_sent, down_kept, down_zz = next_step(down_kept, down_z, rep, 4)
    out_sent, out_kept, out_zz = next_step(out_kept, out_y, rep, 4)
    _, small_kept, small_zz = step(small_kept + small_z, rep, 4, 2)

    b_y = after(b_y, down_sent, out_sent)
    b_sent, b_kept, b_z = next_step(b_kept, b_y, rep, 2)
    a_z, small_zz = after(a_z, b_sent), after(small_zz, b_sent)
    low_zz, high_zz = after(low_zz, b_sent), after(high_zz, b_sent)
    _, a_kept, a_zz = next_step(a_kept, a_z, rep, 4)
    _, small_kept, small_y = step(small_kept + small_zz, rep, 1)
    mid_low = last_steps(low_kept, low_zz, rep)
    mid_high = last_steps(high_kept, high_zz, rep)
    _, b_kept, b_zz = next_step(b_kept, b_z, rep, 4)
    down = last_steps(down_kept, down_zz, rep)
    out_grad = last_steps(out_kept, out_zz, rep)
    in_grad = jnp.concatenate(
        [last_steps(a_kept, a_zz, rep), last_steps(b_kept, b_zz, rep)], axis=1
    )
    small_total = last_steps(small_kept, small_y, rep).reshape(-1)
    smalls_out, start = [], 0
    for part in small_grads:
        smalls_out.append(small_total[start : start + part.shape[2]])
        start += part.shape[2]
    gain_one_out, taps_out, offset_out, gain_mixer_out, gain_two_out, heads_out = smalls_out
    each = HM // 4
    mixer_m = mixer_rows_of // reps
    return (
        output,
        tokens_grad,
        gain_one_out,
        in_grad[:, GATE_AT:MIXED_AT],
        in_grad[:, MIXED_AT:Q_AT],
        in_grad[:, STEP_AT : STEP_AT + HM],
        taps_out.reshape(KC, -1),
        offset_out,
        heads_out[:each],
        heads_out[each : 2 * each],
        heads_out[2 * each :],
        gain_mixer_out,
        out_grad[:mixer_m],
        in_grad[:, Q_AT:K_AT],
        in_grad[:, K_AT:V_AT],
        in_grad[:, V_AT:STEP_AT],
        out_grad[mixer_m:],
        gain_two_out,
        mid_low,
        mid_high,
        down,
    )


def solution(mesh):
    both = P(("shard", "rep"), None)
    rows, vector = P("shard", None), P("shard")
    owned = P(("shard", "rep"))
    return jax.shard_map(
        local,
        mesh=mesh,
        in_specs=(
            both,
            both,
            vector,
            rows,
            rows,
            rows,
            P(None, "shard"),
            vector,
            vector,
            vector,
            vector,
            vector,
            rows,
            rows,
            rows,
            rows,
            rows,
            vector,
            rows,
            rows,
            rows,
        ),
        out_specs=(
            both,
            both,
            owned,
            both,
            both,
            both,
            P(None, ("shard", "rep")),
            owned,
            vector,
            vector,
            vector,
            owned,
            both,
            both,
            both,
            both,
            both,
            owned,
            both,
            both,
            both,
        ),
        check_vma=False,
    )
```

```python
import jax
import jax.numpy as jnp
from jax import lax
from jax.experimental import pallas as pl
from jax.experimental.pallas import tpu as pltpu
from jax.sharding import PartitionSpec as P

QUERY_HEADS = 8
KEY_VALUE_HEADS = 2
HEAD_WIDTH = 64
HM = 24
P_SIZE = 64
N = 128
KC = 4
SEQUENCE_LENGTH = 128
DS = 1536
XBC = 1792
WIDTH = 1024
QW = QUERY_HEADS * HEAD_WIDTH
KW = KEY_VALUE_HEADS * HEAD_WIDTH
GATE_AT, MIXED_AT = 0, DS
Q_AT = MIXED_AT + XBC
K_AT = Q_AT + QW
V_AT = K_AT + KW
STEP_AT = V_AT + KW
IN_COLS = STEP_AT + 128


EPS = 1e-05
HIGH = lax.Precision.HIGHEST
BF = jnp.bfloat16
F32 = jnp.float32


def swap(value, axis, bit):
    size = lax.axis_size(axis)
    return lax.ppermute(value, axis, [(i, i ^ bit) for i in range(size)])


def core(value):
    return swap(value, "shard", 1)


def over_x(value):
    return swap(value, "shard", 2)


def over_y(value):
    return swap(value, "rep", 1)


def over_z(value):
    return swap(value, "rep", 2)


def over_zz(value):
    return swap(value, "rep", 4)


ANY = pl.BlockSpec(memory_space=pltpu.HBM)
VMEM = pl.BlockSpec(memory_space=pltpu.VMEM)
SMEM = pl.BlockSpec(memory_space=pltpu.SMEM)
VMEM_LIMIT = 60 << 20


def call(body, outs, in_specs, scratch, name, flops=0, moved=0):
    return pl.pallas_call(
        body,
        out_shape=[jax.ShapeDtypeStruct(shape, dtype) for shape, dtype in outs],
        in_specs=in_specs,
        out_specs=[VMEM] * len(outs),
        scratch_shapes=scratch,
        compiler_params=pltpu.CompilerParams(vmem_limit_bytes=VMEM_LIMIT),
        name=name,
        cost_estimate=pl.CostEstimate(flops=0, bytes_accessed=0, transcendentals=0),
    )


def run_copies(pairs, sems):
    copies = [
        pltpu.make_async_copy(source, target, sems.at[i]) for i, (source, target) in enumerate(pairs)
    ]
    for copy in copies:
        copy.start()
    for copy in copies:
        copy.wait()


def after(value, *others):
    def body(*refs):
        del refs

    return pl.pallas_call(
        body,
        out_shape=jax.ShapeDtypeStruct(value.shape, value.dtype),
        in_specs=[ANY] * (1 + len(others)),
        out_specs=ANY,
        input_output_aliases={0: 0},
        name="after",
    )(value, *others)


def dot(left, right):
    return jnp.dot(left, right, preferred_element_type=F32)


def dot_rows(left, right):
    return lax.dot_general(left, right, (((1,), (1,)), ((), ())), preferred_element_type=F32)


def dot_tokens(left, right):
    return lax.dot_general(left, right, (((0,), (0,)), ((), ())), preferred_element_type=F32)


def quarter(meta, rows):
    part = rows // 4
    return part, pl.multiple_of((meta[1] & 3) * part, part)


IN_PARTS = (
    (GATE_AT, DS),
    (MIXED_AT, XBC),
    (Q_AT, QW),
    (K_AT, KW),
    (V_AT, KW),
)


def pack_in_quarter(meta, step, mixer_gate, mixer_input, query, key, value):
    rows = step.shape[0]

    def body(meta, step, *refs):
        weights, (target, sems) = refs[:5], refs[5:]
        part, start = quarter(meta, rows)
        target[:, STEP_AT:] = jnp.zeros((part, IN_COLS - STEP_AT), BF)
        target[:, STEP_AT : STEP_AT + HM] = step[pl.ds(start, part), :]
        run_copies(
            [
                (weight.at[pl.ds(start, part)], target.at[:, pl.ds(at, width)])
                for (at, width), weight in zip(IN_PARTS, weights)
            ],
            sems,
        )

    return call(
        body,
        [((rows // 4, IN_COLS), BF)],
        [SMEM, VMEM] + [ANY] * 5,
        [pltpu.SemaphoreType.DMA((5,))],
        "pack_in_quarter",
    )(meta, step, mixer_gate, mixer_input, query, key, value)[0]


def pack_in(step, mixer_gate, mixer_input, query, key, value):
    rows = step.shape[0]

    def body(step, *refs):
        weights, (target, sems) = refs[:5], refs[5:]
        target[:, STEP_AT:] = jnp.zeros((rows, IN_COLS - STEP_AT), BF)
        target[:, STEP_AT : STEP_AT + HM] = step[...]
        run_copies(
            [
                (weight, target.at[:, pl.ds(at, width)])
                for (at, width), weight in zip(IN_PARTS, weights)
            ],
            sems,
        )

    return call(
        body,
        [((rows, IN_COLS), BF)],
        [VMEM] + [ANY] * 5,
        [pltpu.SemaphoreType.DMA((5,))],
        "pack_in",
        moved=4 * rows * IN_COLS,
    )(step, mixer_gate, mixer_input, query, key, value)[0]


OUT_AT, FFN_GATE_AT, FFN_UP_AT, DOWN_AT = 0, 2048, 4096, 6144
REST_COLS = 8192


def pack_rest(meta, behind, mixer_output, attn_output, gate, up, down):
    rows = gate.shape[0]
    half = rows // 2

    def body(meta, behind, mixer_output, attn_output, gate, up, down, target, first, sems):
        def block(at, width=WIDTH):
            return target.at[:, pl.ds(at, width)]

        low = target.at[pl.ds(0, half), pl.ds(OUT_AT + WIDTH, WIDTH)]
        high = target.at[pl.ds(half, half), pl.ds(OUT_AT + WIDTH, WIDTH)]
        pairs = [
            (mixer_output.at[pl.ds(0, rows)], block(OUT_AT)),
            (gate, block(FFN_GATE_AT, 2048)),
            (up, block(FFN_UP_AT, 2048)),
            (down.at[pl.ds(0, rows)], block(DOWN_AT)),
            (down.at[pl.ds(rows, rows)], block(DOWN_AT + WIDTH)),
            (mixer_output.at[pl.ds(rows, half)], low),
            (attn_output, high),
        ]
        run_copies(pairs, sems)
        part, start = quarter(meta, rows)
        first[...] = target[pl.ds(start, part), :]

    return call(
        body,
        [((rows, REST_COLS), BF), ((rows // 4, REST_COLS), BF)],
        [SMEM] + [ANY] * 6,
        [pltpu.SemaphoreType.DMA((7,))],
        "pack_rest",
    )(meta, behind, mixer_output, attn_output, gate, up, down)


def spread(packed, near, first, last):
    half = first.shape[0] // 2
    from_y, from_z = over_y(first), over_z(first)
    low, high = over_y(from_z[:half]), over_z(from_y[half:])
    far = (first, from_y, from_z, after(low, last), after(high, last))
    return (packed, near) + far + tuple(core(piece) for piece in far)


def spread_first(first, *others):
    first = after(first, *others)
    return first, over_y(first), over_z(first)


def spread_last(packed, near, parts, middle, end):
    first, from_y, from_z = parts
    half = first.shape[0] // 2
    from_y, from_z = after(from_y, middle), after(from_z, middle)
    low, high = over_y(from_z[:half]), over_z(from_y[half:])
    far = (first, from_y, from_z, low, high)
    others = tuple(core(piece) for piece in far[:3])
    low, high = after(low, end), after(high, end)
    return (packed, near, first, from_y, from_z, low, high) + others + (core(low), core(high))


def fill(meta, pieces, target, sems):
    shard, mine = meta[0], meta[1] & 3
    rows = pieces[0].shape[0]
    part = rows // 4
    pairs = [
        (pieces[0], target.at[pl.ds(pl.multiple_of(shard * rows, rows), rows)]),
        (pieces[1], target.at[pl.ds(pl.multiple_of((shard ^ 1) * rows, rows), rows)]),
    ]
    for at, owner in ((2, shard ^ 2), (7, shard ^ 3)):
        for j, add in enumerate((0, 0, 0, 0, part // 2)):
            start = pl.multiple_of(owner * rows + (mine ^ min(j, 3)) * part + add, part // 2)
            size = part if j < 3 else part // 2
            pairs.append((pieces[at + j], target.at[pl.ds(start, size)]))
    run_copies(pairs, sems)


PIECES = 12
MIX_SHARD, ATT_SHARD, FF_SHARD, W_SHARD = DS // 4, QW // 4, 512, WIDTH // 4
OUT_SHARD = MIX_SHARD + ATT_SHARD


def columns_of(ref, shard, width):
    return ref[:, pl.ds(pl.multiple_of(shard * width, 128), width)]


NORM_AT = 4096 + WIDTH
ACT_AT_X, ACT_AT_CORE = NORM_AT + 2 * W_SHARD, NORM_AT + W_SHARD


def columns_for_others(shard, ref, width, to_x, to_core, at=0, at_core=0):
    to_x[:, at : at + width] = columns_of(ref, shard ^ 2, width)
    to_x[:, at + width : at + 2 * width] = columns_of(ref, shard ^ 3, width)
    to_core[:, at_core : at_core + width] = columns_of(ref, shard ^ 1, width)


def norm_rate(value):
    return lax.rsqrt(jnp.mean(value * value, axis=-1, keepdims=True) + EPS)


def norm_back(value, rate, gain, grad):
    scaled = gain * grad
    grad_value = rate * scaled - value * (rate * rate * rate) * jnp.mean(
        value * scaled, axis=-1, keepdims=True
    )
    return grad_value, jnp.sum(value * rate * grad, axis=0, keepdims=True)


def project_in(meta, tokens, gain, pieces):
    def body(meta, tokens, gain, *refs):
        pieces, (normed_ref, to_x, to_core, out, weight, sems) = refs[:PIECES], refs[PIECES:]
        fill(meta, pieces, weight, sems)
        value = tokens[...].astype(F32)
        normed = (value * norm_rate(value) * gain[...]).astype(BF)
        normed_ref[...] = normed
        columns_for_others(meta[0], normed_ref, W_SHARD, to_x, to_core)
        out[...] = dot(normed, weight[...])

    rows = tokens.shape[0]
    return call(
        body,
        [
            ((rows, WIDTH), BF),
            ((rows, 2 * W_SHARD), BF),
            ((rows, W_SHARD), BF),
            ((rows, IN_COLS), F32),
        ],
        [SMEM, VMEM, VMEM] + [ANY] * PIECES,
        [pltpu.VMEM((WIDTH, IN_COLS), BF), pltpu.SemaphoreType.DMA((PIECES,))],
        "project_in",
        flops=2 * rows * WIDTH * IN_COLS,
        moved=2 * WIDTH * IN_COLS,
    )(meta, tokens, gain, *pieces)


def project_in_back(meta, tokens, gain, grad_projected, grad_middle, pieces):
    def body(meta, tokens, gain, grad_projected, grad_middle, *refs):
        pieces, (out, grad_gain, weight, sems) = refs[:PIECES], refs[PIECES:]
        fill(meta, pieces, weight, sems)
        value = tokens[...].astype(F32)
        rate = norm_rate(value)
        grad = dot_rows(grad_projected[:, :IN_COLS], weight[...])
        grad_value, grad_gain[...] = norm_back(value, rate, gain[...], grad)
        out[...] = (grad_middle[...] + grad_value).astype(BF)

    rows = tokens.shape[0]
    return call(
        body,
        [((rows, WIDTH), BF), ((1, WIDTH), F32)],
        [SMEM] + [VMEM] * 4 + [ANY] * PIECES,
        [pltpu.VMEM((WIDTH, IN_COLS), BF), pltpu.SemaphoreType.DMA((PIECES,))],
        "project_in_back",
        flops=2 * rows * WIDTH * IN_COLS,
        moved=2 * WIDTH * IN_COLS,
    )(meta, tokens, gain, grad_projected, grad_middle, *pieces)


def silu_parts(value):
    share = 1.0 / (1.0 + jnp.exp(-value))
    return value * share, share


def silu_slope(value, share):
    return share * (1.0 + value * (1.0 - share))


def exact(left, right, axes=((1,), (0,))):
    return lax.dot_general(
        left, right, (axes, ((), ())), precision=HIGH, preferred_element_type=F32
    )


def causal_mask(rows):
    return lax.broadcasted_iota(jnp.int32, (rows, rows), 0) >= lax.broadcasted_iota(
        jnp.int32, (rows, rows), 1
    )


EDGE = 8


def mixer_state(projected, taps, offset, step_offset, decay, padded, causal):
    rows = projected.shape[0]
    padded[:EDGE] = jnp.zeros((EDGE, XBC), F32)
    padded[EDGE:] = projected[:, MIXED_AT:Q_AT]
    convolved = offset[...]
    for o in range(KC):
        start = EDGE - KC + 1 + o
        convolved = convolved + padded[start : start + rows] * taps[o : o + 1]
    active, share = silu_parts(convolved)
    raw = projected[:, STEP_AT:] + step_offset[...]
    step = jnp.maximum(raw, 0.0) + jnp.log1p(jnp.exp(-jnp.abs(raw)))
    rate = jnp.exp(decay[...])
    log_decay = -step * rate
    running = exact(causal.astype(F32), log_decay)
    return convolved, active, share, raw, step, rate, log_decay, running


def decay_of(running, running_t, causal, h):
    spread = running[:, h : h + 1] - running_t[h : h + 1]
    return jnp.where(causal, jnp.exp(jnp.where(causal, spread, 0.0)), 0.0)


def head(value, h):
    return value[:, h * HEAD_WIDTH : (h + 1) * HEAD_WIDTH]


def shares_of(query, key, causal):
    scores = jnp.where(causal, dot_rows(query, key) * HEAD_WIDTH ** (-0.5), -1e30)
    unscaled = jnp.exp(scores - jnp.max(scores, axis=-1, keepdims=True))
    return unscaled / jnp.sum(unscaled, axis=-1, keepdims=True)


def mix(meta, projected, taps, offset, step_offset, decay, skip, gain):
    rows = projected.shape[0]

    def body(meta, projected, taps, offset, step_offset, decay, skip, gain, *refs):
        side, to_x, to_core, result_ref, padded, active_ref = refs
        causal = causal_mask(rows)
        _, active, _, _, step, _, _, running = mixer_state(
            projected, taps, offset, step_offset, decay, padded, causal
        )
        active_ref[...] = active
        running_t, step_t = running.T, step.T
        coupling = exact(active[:, DS + N :], active[:, DS : DS + N], ((1,), (1,)))
        for h in range(HM):
            mixing = coupling * decay_of(running, running_t, causal, h) * step_t[h : h + 1]
            at = h * P_SIZE
            result_ref[:, at : at + P_SIZE] = exact(mixing, active_ref[:, at : at + P_SIZE])
        result = result_ref[...] + skip[...] * active_ref[:, :DS]
        gated = result * silu_parts(projected[:, GATE_AT:MIXED_AT])[0]
        mixed = (gated * norm_rate(gated) * gain[...]).astype(BF)
        for k in range(4):
            side[:, k * OUT_SHARD : k * OUT_SHARD + MIX_SHARD] = mixed[
                :, k * MIX_SHARD : (k + 1) * MIX_SHARD
            ]
        for h in range(QUERY_HEADS):
            query = projected[:, Q_AT + h * HEAD_WIDTH : Q_AT + (h + 1) * HEAD_WIDTH]
            at = (h // (QUERY_HEADS // KEY_VALUE_HEADS)) * HEAD_WIDTH
            key = projected[:, K_AT + at : K_AT + at + HEAD_WIDTH]
            value = projected[:, V_AT + at : V_AT + at + HEAD_WIDTH]
            shares = shares_of(query.astype(BF), key.astype(BF), causal)
            at = (h // 2) * OUT_SHARD + MIX_SHARD + (h % 2) * HEAD_WIDTH
            side[:, at : at + HEAD_WIDTH] = dot(shares.astype(BF), value.astype(BF)).astype(BF)
        columns_for_others(meta[0], side, OUT_SHARD, to_x, to_core)

    return call(
        body,
        [((rows, 4 * OUT_SHARD), BF), ((rows, 2 * OUT_SHARD), BF), ((rows, OUT_SHARD), BF)],
        [SMEM] + [VMEM] * 7,
        [
            pltpu.VMEM((rows, DS), F32),
            pltpu.VMEM((EDGE + rows, XBC), F32),
            pltpu.VMEM((rows, XBC), F32),
        ],
        "mix",
    )(meta, projected, taps, offset, step_offset, decay, skip, gain)


def mix_back(projected, taps, offset, step_offset, decay, skip, gain, grad_norm, grad_ctx):
    rows = projected.shape[0]

    def body(projected, taps, offset, step_offset, decay, skip, gain, grad_norm, grad_ctx, *refs):
        (
            to_core,
            grad_gain,
            grad_taps,
            grad_offset,
            grad_step_offset,
            grad_decay,
            grad_skip,
            result_ref,
            padded,
            active_ref,
            grad_active,
            column_ref,
            row_ref,
        ) = refs
        causal = causal_mask(rows)
        convolved, active, share, raw, step, rate, log_decay, running = mixer_state(
            projected, taps, offset, step_offset, decay, padded, causal
        )
        active_ref[...] = active
        running_t, step_t = running.T, step.T
        in_state, out_state = active[:, DS : DS + N], active[:, DS + N :]
        coupling = exact(out_state, in_state, ((1,), (1,)))
        for h in range(HM):
            mixing = coupling * decay_of(running, running_t, causal, h) * step_t[h : h + 1]
            at = h * P_SIZE
            result_ref[:, at : at + P_SIZE] = exact(mixing, active_ref[:, at : at + P_SIZE])
        inner = active_ref[:, :DS]
        result = result_ref[...] + skip[...] * inner
        gate = projected[:, GATE_AT:MIXED_AT]
        silu, gate_share = silu_parts(gate)
        gated = result * silu
        grad_gated, grad_gain[...] = norm_back(gated, norm_rate(gated), gain[...], grad_norm[...])
        to_core[:, GATE_AT:MIXED_AT] = (
            grad_gated * result * silu_slope(gate, gate_share)
        ).astype(BF)
        grad_result = grad_gated * silu
        result_ref[...] = grad_result
        grad_skip[...] = jnp.sum(grad_result * inner, axis=0, keepdims=True)
        grad_coupling = jnp.zeros((rows, rows), F32)
        column_ref[...] = jnp.zeros_like(column_ref)
        row_ref[...] = jnp.zeros_like(row_ref)
        for h in range(HM):
            at = h * P_SIZE
            decays = decay_of(running, running_t, causal, h)
            step_row = step_t[h : h + 1]
            scaled = decays * step_row
            grad_out = result_ref[:, at : at + P_SIZE]
            grad_active[:, at : at + P_SIZE] = exact(coupling * scaled, grad_out, ((0,), (0,)))
            grad_mixing = exact(grad_out, active_ref[:, at : at + P_SIZE], ((1,), (1,)))
            grad_coupling = grad_coupling + grad_mixing * scaled
            weighed = grad_mixing * decays * coupling
            row_ref[h : h + 1] = jnp.sum(weighed, axis=0, keepdims=True)
            column_ref[:, h : h + 1] = jnp.sum(weighed * step_row, axis=1, keepdims=True)
        grad_active[:, :DS] = grad_active[:, :DS] + skip[...] * result_ref[...]
        grad_active[:, DS : DS + N] = exact(grad_coupling, out_state, ((0,), (0,)))
        grad_active[:, DS + N :] = exact(grad_coupling, in_state)
        grad_step = row_ref[...].T
        grad_running = column_ref[...] - grad_step * step
        grad_log = exact(causal.astype(F32), grad_running, ((0,), (0,)))
        grad_decay[...] = jnp.sum(grad_log * log_decay, axis=0, keepdims=True)
        grad_raw = (grad_step - grad_log * rate) / (1.0 + jnp.exp(-raw))
        grad_step_offset[...] = jnp.sum(grad_raw, axis=0, keepdims=True)
        lanes = lax.broadcasted_iota(jnp.int32, (rows, 128), 1)
        to_core[:, STEP_AT:IN_COLS] = jnp.where(lanes < HM, grad_raw, 0.0).astype(BF)
        grad_conv = grad_active[...] * silu_slope(convolved, share)
        grad_offset[...] = jnp.sum(grad_conv, axis=0, keepdims=True)
        for o in range(KC):
            start = EDGE - KC + 1 + o
            grad_taps[o : o + 1] = jnp.sum(
                grad_conv * padded[start : start + rows], axis=0, keepdims=True
            )
        padded[:rows] = grad_conv
        padded[rows:] = jnp.zeros((EDGE, XBC), F32)
        grad_mixed = grad_conv * taps[KC - 1 : KC]
        for o in range(KC - 1):
            start = KC - 1 - o
            grad_mixed = grad_mixed + padded[start : start + rows] * taps[o : o + 1]
        to_core[:, MIXED_AT:Q_AT] = grad_mixed.astype(BF)

        group = QUERY_HEADS // KEY_VALUE_HEADS
        for kv in range(KEY_VALUE_HEADS):
            at = kv * HEAD_WIDTH
            key = projected[:, K_AT + at : K_AT + at + HEAD_WIDTH].astype(BF)
            value = projected[:, V_AT + at : V_AT + at + HEAD_WIDTH].astype(BF)
            grad_key = jnp.zeros((rows, HEAD_WIDTH), F32)
            grad_value = jnp.zeros((rows, HEAD_WIDTH), F32)
            for h in range(kv * group, (kv + 1) * group):
                query = projected[:, Q_AT + h * HEAD_WIDTH : Q_AT + (h + 1) * HEAD_WIDTH]
                query = query.astype(BF)
                shares = shares_of(query, key, causal)
                given = grad_ctx[:, h * HEAD_WIDTH : (h + 1) * HEAD_WIDTH]
                grad_shares = dot_rows(given, value)
                grad_value = grad_value + dot_tokens(shares.astype(BF), given)
                weighed = shares * grad_shares
                grad_scores = weighed - shares * jnp.sum(weighed, axis=-1, keepdims=True)
                grad_scores = (grad_scores * HEAD_WIDTH ** (-0.5)).astype(BF)
                to_core[:, Q_AT + h * HEAD_WIDTH : Q_AT + (h + 1) * HEAD_WIDTH] = dot(
                    grad_scores, key
                ).astype(BF)
                grad_key = grad_key + dot_tokens(grad_scores, query)
            to_core[:, K_AT + at : K_AT + at + HEAD_WIDTH] = grad_key.astype(BF)
            to_core[:, V_AT + at : V_AT + at + HEAD_WIDTH] = grad_value.astype(BF)
    return call(
        body,
        [
            ((rows, IN_COLS), BF),
            ((1, DS), F32),
            ((KC, XBC), F32),
            ((1, XBC), F32),
            ((1, 128), F32),
            ((1, 128), F32),
            ((1, DS), F32),
        ],
        [VMEM] * 9,
        [
            pltpu.VMEM((rows, DS), F32),
            pltpu.VMEM((EDGE + rows, XBC), F32),
            pltpu.VMEM((rows, XBC), F32),
            pltpu.VMEM((rows, XBC), F32),
            pltpu.VMEM((rows, 128), F32),
            pltpu.VMEM((128, rows), F32),
        ],
        "mix_back",
    )(projected, taps, offset, step_offset, decay, skip, gain, grad_norm, grad_ctx)


def feed_forward(meta, tokens, cotangent, side, gain, pieces):
    def body(meta, tokens, cotangent, side, gain, *refs):
        pieces, refs = refs[:PIECES], refs[PIECES:]
        (
            output,
            normed_ref,
            act_ref,
            grad_middle_ref,
            grad_norm_ref,
            grad_context_ref,
            grad_gain,
            to_x,
            mid_core,
            weight,
            sems,
        ) = refs
        fill(meta, pieces, weight, sems)
        shard = meta[0]

        def block(at):
            return weight[:, at : at + WIDTH]

        def half_of(ref, h):
            return jnp.concatenate(
                [ref[:, k * 512 + h * 256 : k * 512 + h * 256 + 256] for k in range(4)], axis=1
            )

        middle = tokens[...].astype(F32)
        for h in range(2):
            middle = middle + dot(half_of(side, h), block(OUT_AT + h * WIDTH))
        rate = norm_rate(middle)
        normed = (middle * rate * gain[...]).astype(BF)
        normed_ref[...] = normed
        given = cotangent[...]
        added = []
        grad_normed = jnp.zeros_like(middle)
        for h in range(2):
            down = block(DOWN_AT + h * WIDTH)
            grad_act = dot_rows(given, down)
            for k in range(4):
                at = k * 512 + h * 256
                gate = dot(normed, weight[:, FFN_GATE_AT + at : FFN_GATE_AT + at + 256])
                up = dot(normed, weight[:, FFN_UP_AT + at : FFN_UP_AT + at + 256])
                share = 1.0 / (1.0 + jnp.exp(-gate))
                silu = gate * share
                act = (silu * up).astype(BF)
                act_ref[:, at : at + 256] = act
                grad = grad_act[:, k * 256 : (k + 1) * 256]
                mid_core[:, at : at + 256] = (
                    grad * up * share * (1.0 + gate * (1.0 - share))
                ).astype(BF)
                mid_core[:, 2048 + at : 2048 + at + 256] = (grad * silu).astype(BF)
            added.append(dot(half_of(act_ref, h), down))
        output[...] = (middle + (added[0] + added[1])).astype(BF)
        for j in range(4):
            at = j * WIDTH
            grad_normed = grad_normed + dot_rows(
                mid_core[:, at : at + WIDTH], block(FFN_GATE_AT + at)
            )
        grad_value, grad_gain[...] = norm_back(middle, rate, gain[...], grad_normed)
        grad_middle = given.astype(F32) + grad_value
        grad_middle_ref[...] = grad_middle
        branch = grad_middle.astype(BF)
        for h in range(2):
            grad = dot_rows(branch, block(OUT_AT + h * WIDTH))
            for k in range(4):
                at = k * MIX_SHARD + h * 256
                piece = grad[:, k * 256 : (k + 1) * 256]
                if h == 0:
                    grad_norm_ref[:, at : at + 256] = piece
                else:
                    grad_norm_ref[:, at : at + 128] = piece[:, :128]
                    grad_context_ref[:, k * 128 : (k + 1) * 128] = piece[:, 128:].astype(BF)
        mid_core[:, 4096 : 4096 + WIDTH] = branch
        to_x[:, : 4096 + WIDTH] = mid_core[:, : 4096 + WIDTH]
        columns_for_others(shard, normed_ref, W_SHARD, to_x, mid_core, NORM_AT, NORM_AT)
        columns_for_others(shard, act_ref, FF_SHARD, to_x, mid_core, ACT_AT_X, ACT_AT_CORE)

    rows = tokens.shape[0]
    return call(
        body,
        [
            ((rows, WIDTH), BF),
            ((rows, WIDTH), BF),
            ((rows, 2048), BF),
            ((rows, WIDTH), F32),
            ((rows, DS), F32),
            ((rows, QW), BF),
            ((1, WIDTH), F32),
            ((rows, ACT_AT_X + 2 * FF_SHARD), BF),
            ((rows, ACT_AT_CORE + FF_SHARD), BF),
        ],
        [SMEM] + [VMEM] * 4 + [ANY] * PIECES,
        [pltpu.VMEM((WIDTH, REST_COLS), BF), pltpu.SemaphoreType.DMA((PIECES,))],
        "feed_forward",
        flops=4 * rows * WIDTH * REST_COLS,
        moved=2 * WIDTH * REST_COLS,
    )(meta, tokens, cotangent, side, gain, *pieces)


def exchange(to_x, to_core):
    far = over_x(to_x)
    return core(to_core), far, core(far)


def weight_products(meta, groups, name, cuts=(0,)):
    tokens = groups[0][3].shape[0]
    arrays = []

    def slot(array):
        for i, known in enumerate(arrays):
            if known is array:
                return i
        arrays.append(array)
        return len(arrays) - 1

    plan = [
        (
            width,
            w,
            [(slot(a), at) for a, at in grads],
            slot(own),
            [(slot(a), at) for a, at in others],
        )
        for width, w, grads, own, others in groups
    ]
    count, many = len(arrays), len(plan)
    pieces = [
        (i, at, end)
        for i, (width, *_) in enumerate(plan)
        for at, end in zip(cuts, cuts[1:] + (width,))
    ]

    def body(meta, *refs):
        sources, refs = refs[:count], refs[count:]
        outs, refs = refs[: len(pieces)], refs[len(pieces) :]
        lefts, rights, sems = refs[:many], refs[many : 2 * many], refs[2 * many]
        pairs = []
        for (width, w, grads, own, others), left, right in zip(plan, lefts, rights):
            at_own = pl.multiple_of(meta[0] * w, 128)
            columns = [(own, at_own)] + others
            for i in range(4):
                here = pl.ds(i * tokens, tokens)
                source, at = grads[i]
                pairs.append((sources[source].at[:, pl.ds(at, width)], right.at[here]))
                source, at = columns[i]
                pairs.append((sources[source].at[:, pl.ds(at, w)], left.at[here]))
        run_copies(pairs, sems)
        for out, (i, start, end) in zip(outs, pieces):
            turned, right = lefts[i][...], rights[i]
            for j in range(start, end, 256):
                step = min(256, end - j)
                out[:, j - start : j - start + step] = dot_tokens(
                    turned, right[:, j : j + step]
                ).astype(BF)

    return call(
        body,
        [((plan[i][1], end - start), BF) for i, start, end in pieces],
        [SMEM] + [ANY] * count,
        [pltpu.VMEM((4 * tokens, w), BF) for _, w, *_ in plan]
        + [pltpu.VMEM((4 * tokens, width), BF) for width, *_ in plan]
        + [pltpu.SemaphoreType.DMA((8 * many,))],
        name,
    )(meta, *arrays)


def bit_of(index, bit):
    return (index // bit) & 1


def halve(total, rep, bit, below=1):
    split = total.reshape((total.shape[0] // (2 * below), 2, below) + total.shape[1:])
    mine = bit_of(rep, bit)
    return tuple(
        lax.dynamic_index_in_dim(split, j, 1, keepdims=False).reshape((-1,) + total.shape[1:])
        for j in (1 - mine, mine)
    )


def add(kept, arrived):
    return kept.astype(F32) + arrived.astype(F32)


def step(total, rep, bit, below=1):
    sent, kept = halve(total, rep, bit, below)
    return sent, kept, swap(sent, "rep", bit)


def next_step(kept, arrived, rep, bit):
    return step(add(kept, arrived).astype(BF), rep, bit)


def last_steps(kept, arrived, rep, bit=8):
    total, held = add(kept, arrived), kept.dtype
    while bit < lax.axis_size("rep"):
        total = add(*step(total.astype(held), rep, bit)[1:])
        bit *= 2
    return total.reshape(-1, total.shape[-1])


def pick_bit(blocks, axis, bit):
    return tuple(
        lax.dynamic_index_in_dim(blocks, j, axis, keepdims=False) for j in (1 - bit, bit)
    )


def local(
    tokens,
    cotangent,
    first_gain,
    mixer_gate,
    mixer_input,
    step_weight,
    conv_weight,
    conv_bias,
    step_bias,
    decay_log,
    skip_weight,
    mixer_gain,
    mixer_output,
    query_matrix,
    key_matrix,
    value_matrix,
    attn_output,
    second_gain,
    ffn_gate,
    ffn_up,
    ffn_down,
):
    shard = lax.axis_index("shard")
    rep = lax.axis_index("rep")
    reps = lax.axis_size("rep")

    small_parts = (
        first_gain,
        conv_weight.reshape(-1),
        conv_bias,
        step_bias,
        decay_log,
        skip_weight,
        mixer_gain,
        second_gain,
    )
    small = jnp.concatenate(small_parts)
    small = jnp.pad(small, (0, -small.shape[0] % 128)).reshape(1, -1)
    far_small = over_x(small)
    smalls = jnp.concatenate([small, core(small), far_small, core(far_small)], axis=0)
    smalls = jnp.take(smalls, jnp.arange(4) ^ shard, axis=0).astype(F32)
    full, at = [], 0
    for part in small_parts:
        full.append(smalls[:, at : at + part.shape[0]])
        at += part.shape[0]
    taps = full[1].reshape(4, KC, -1).transpose(1, 0, 2).reshape(KC, XBC)
    gain_one, offset, step_offset, decay_rates, skip_scale, gain_mixer, gain_two = (
        full[i].reshape(-1) for i in (0, 2, 3, 4, 5, 6, 7)
    )

    meta = jnp.stack([shard, rep]).astype(jnp.int32)
    in_weights = (step_weight, mixer_gate, mixer_input, query_matrix, key_matrix, value_matrix)
    in_first = pack_in_quarter(meta, *in_weights)
    rest_packed, rest_first = pack_rest(
        meta, in_first, mixer_output, attn_output, ffn_gate, ffn_up, ffn_down
    )
    in_packed = pack_in(*in_weights)
    in_first = over_x(in_first)
    rest_first = over_x(after(rest_first, in_first, far_small))
    in_pieces = spread(in_packed, core(in_packed), in_first, rest_first)
    mixer_rows_of = DS // 4
    ff = 2048

    gain_one, gain_two = gain_one.reshape(1, -1), gain_two.reshape(1, -1)
    normalized_input, norm_x, norm_core, projected = project_in(
        meta, tokens, gain_one, in_pieces
    )
    rest_near = core(rest_packed)
    rest_parts = spread_first(rest_first, *in_pieces[5:7])
    def lanes(vector):
        return jnp.pad(vector, (0, 128 - HM)).reshape(1, 128)

    mixer_small = (
        taps,
        offset.reshape(1, -1),
        lanes(step_offset),
        lanes(decay_rates),
        jnp.repeat(skip_scale, P_SIZE).reshape(1, -1),
        gain_mixer.reshape(1, -1),
    )
    side, side_x, side_core = mix(meta, projected, *mixer_small)
    rest_pieces = spread_last(rest_packed, rest_near, rest_parts, normalized_input, side)
    (
        output,
        normed_two,
        activated,
        grad_middle,
        grad_mixer_norm,
        grad_context,
        grad_gain_two,
        mid_x,
        mid_core,
    ) = feed_forward(
        meta, tokens, cotangent, side, gain_two, rest_pieces
    )
    given = cotangent
    given_others = exchange(given, given)
    norm_others = exchange(norm_x, norm_core)
    side_others = exchange(side_x, side_core)
    early = (given_others[1], norm_others[1], side_others[1])
    mid_far = over_x(after(mid_x, *early))
    (
        in_own,
        grad_gain_mixer,
        grad_taps,
        grad_offset,
        grad_step_offset,
        grad_decay,
        grad_skip,
    ) = mix_back(projected, *mixer_small, grad_mixer_norm, grad_context)
    tokens_grad, grad_gain_one = project_in_back(
        meta, tokens, gain_one, in_own, grad_middle, in_pieces
    )
    mid_far = after(mid_far, in_own, tokens_grad)
    grad_step_offset, grad_decay = grad_step_offset[0, :HM], grad_decay[0, :HM]
    grad_skip = grad_skip.reshape(HM, P_SIZE).sum(axis=1)
    def blocks(vector):
        return vector.reshape(4, reps, -1)

    heads = jnp.concatenate(
        [grad_step_offset.reshape(4, -1), grad_decay.reshape(4, -1), grad_skip.reshape(4, -1)],
        axis=1,
    )
    small_grads = (
        blocks(grad_gain_one),
        grad_taps.reshape(KC, 4, reps, -1).transpose(1, 2, 0, 3).reshape(4, reps, -1),
        blocks(grad_offset),
        blocks(grad_gain_mixer),
        blocks(grad_gain_two),
        jnp.broadcast_to(heads[:, None, :], (4, reps, heads.shape[1])),
    )
    small = jnp.concatenate(small_grads, axis=2)
    small = small.reshape((2, 2) + small.shape[1:])
    sent, small_kept = pick_bit(small, 1, bit_of(shard, 1))
    small_core = core(sent)

    def at(arrays, *offsets):
        return list(zip(arrays, offsets))

    mid_others = (core(mid_core), mid_far, core(mid_far))
    in_far = over_x(in_own)
    mid_all = (mid_core,) + mid_others
    mid_low, mid_high = weight_products(
        meta,
        [
            (
                4096,
                W_SHARD,
                at(mid_all, 0, 0, 0, 0),
                normed_two,
                at(mid_others, NORM_AT, NORM_AT, NORM_AT + W_SHARD),
            )
        ],
        "mid_products",
        (0, 2048),
    )
    low_sent, low_kept, low_y = step(mid_low.reshape(reps, -1, 2048), rep, 1)
    high_sent, high_kept, high_z = step(mid_high.reshape(reps, -1, 2048), rep, 2, 2)
    down_blocks, out_blocks = weight_products(
        meta,
        [
            (
                WIDTH,
                FF_SHARD,
                at((given,) + given_others, 0, 0, 0, 0),
                activated,
                at(mid_others, ACT_AT_CORE, ACT_AT_X, ACT_AT_X + FF_SHARD),
            ),
            (
                WIDTH,
                OUT_SHARD,
                at(mid_all, 4096, 4096, 4096, 4096),
                side,
                at(side_others, 0, 0, OUT_SHARD),
            ),
        ],
        "rest_products",
    )
    out_blocks = jnp.concatenate(
        [
            out_blocks[:mixer_rows_of].reshape(reps, -1, WIDTH),
            out_blocks[mixer_rows_of:].reshape(reps, -1, WIDTH),
        ],
        axis=1,
    )
    down_sent, down_kept, down_y = step(down_blocks.reshape(reps, -1, WIDTH), rep, 1)
    out_sent, out_kept, out_z = step(out_blocks, rep, 2, 2)

    low_y = after(low_y, high_z, small_core)
    in_far = after(in_far, low_y, down_sent, out_sent)
    _, low_kept, low_z = next_step(low_kept, low_y, rep, 2)
    _, high_kept, high_y = next_step(high_kept, high_z, rep, 1)
    small_core = after(small_core, in_far)
    sent, small_kept = pick_bit(small_kept + small_core, 0, bit_of(shard, 2))
    small_x = over_x(sent)
    in_others = (core(in_own), in_far, core(in_far))
    in_cut = 2048
    in_low, in_high = weight_products(
        meta,
        [
            (
                IN_COLS,
                W_SHARD,
                at((in_own,) + in_others, 0, 0, 0, 0),
                normalized_input,
                at(norm_others, 0, 0, W_SHARD),
            )
        ],
        "in_products",
        (0, in_cut),
    )
    a_sent, a_kept, a_y = step(in_low.reshape(reps, -1, in_cut), rep, 1)
    b_sent, b_kept, b_one = step(in_high.reshape(reps, -1, IN_COLS - in_cut), rep, 2, 2)

    down_y, out_z = after(down_y, a_sent, b_sent), after(out_z, a_sent, b_sent)
    low_z, high_y = after(low_z, a_sent, b_sent), after(high_y, a_sent, b_sent)
    small_x = after(small_x, a_sent, b_sent)
    down_sent, down_kept, down_z = next_step(down_kept, down_y, rep, 2)
    out_sent, out_kept, out_y = next_step(out_kept, out_z, rep, 1)
    low_sent, low_kept, low_zz = next_step(low_kept, low_z, rep, 4)
    high_sent, high_kept, high_zz = next_step(high_kept, high_y, rep, 4)
    _, small_kept, small_z = step((small_kept + small_x)[:, None], rep, 2, 2)

    a_y = after(a_y, down_sent, out_sent, low_sent, high_sent)
    a_sent, a_kept, a_z = next_step(a_kept, a_y, rep, 2)
    down_z, out_y, small_z = after(down_z, a_sent), after(out_y, a_sent), after(small_z, a_sent)
    down_sent, down_kept, down_zz = next_step(down_kept, down_z, rep, 4)
    out_sent, out_kept, out_zz = next_step(out_kept, out_y, rep, 4)
    _, small_kept, small_zz = step(small_kept + small_z, rep, 4, 2)

    b_one = after(b_one, down_sent, out_sent)
    b_sent, b_kept, b_two = next_step(b_kept, b_one, rep, 1)
    a_z, small_zz = after(a_z, b_sent), after(small_zz, b_sent)
    low_zz, high_zz = after(low_zz, b_sent), after(high_zz, b_sent)
    _, a_kept, a_zz = next_step(a_kept, a_z, rep, 4)
    _, small_kept, small_y = step(small_kept + small_zz, rep, 1)
    mid_low = last_steps(low_kept, low_zz, rep)
    mid_high = last_steps(high_kept, high_zz, rep)
    _, b_kept, b_zz = next_step(b_kept, b_two, rep, 4)
    down = last_steps(down_kept, down_zz, rep)
    out_grad = last_steps(out_kept, out_zz, rep)
    in_grad = jnp.concatenate(
        [last_steps(a_kept, a_zz, rep), last_steps(b_kept, b_zz, rep)], axis=1
    )
    small_total = last_steps(small_kept, small_y, rep).reshape(-1)
    smalls_out, start = [], 0
    for part in small_grads:
        smalls_out.append(small_total[start : start + part.shape[2]])
        start += part.shape[2]
    gain_one_out, taps_out, offset_out, gain_mixer_out, gain_two_out, heads_out = smalls_out
    each = HM // 4
    mixer_m = mixer_rows_of // reps
    return (
        output,
        tokens_grad,
        gain_one_out,
        in_grad[:, GATE_AT:MIXED_AT],
        in_grad[:, MIXED_AT:Q_AT],
        in_grad[:, STEP_AT : STEP_AT + HM],
        taps_out.reshape(KC, -1),
        offset_out,
        heads_out[:each],
        heads_out[each : 2 * each],
        heads_out[2 * each :],
        gain_mixer_out,
        out_grad[:mixer_m],
        in_grad[:, Q_AT:K_AT],
        in_grad[:, K_AT:V_AT],
        in_grad[:, V_AT:STEP_AT],
        out_grad[mixer_m:],
        gain_two_out,
        mid_low,
        mid_high,
        down,
    )


def solution(mesh):
    both = P(("shard", "rep"), None)
    rows, vector = P("shard", None), P("shard")
    owned = P(("shard", "rep"))
    return jax.shard_map(
        local,
        mesh=mesh,
        in_specs=(
            both,
            both,
            vector,
            rows,
            rows,
            rows,
            P(None, "shard"),
            vector,
            vector,
            vector,
            vector,
            vector,
            rows,
            rows,
            rows,
            rows,
            rows,
            vector,
            rows,
            rows,
            rows,
        ),
        out_specs=(
            both,
            both,
            owned,
            both,
            both,
            both,
            P(None, ("shard", "rep")),
            owned,
            vector,
            vector,
            vector,
            owned,
            both,
            both,
            both,
            both,
            both,
            owned,
            both,
            both,
            both,
        ),
        check_vma=False,
    )
```
